32 devices in a mesh: groups: 2 (over y), gx: 4 (over z), gy: 4 (over x, core).
Axes of the slice: x: 2, y: 2, z: 4, core: 2. Of those that a mesh axis runs over, the one named last changes fastest.
Arguments:
- tokens: bfloat16 [2, 384, 8192], P(None, ('groups', 'gy'), 'gx'), parts along dimension 1, may hold values from -6 to 6
- gate_weight: bfloat16 [8192, 26624], P('gx', 'gy'), may hold values from -0.0625 to 0.0625
- up_weight: bfloat16 [8192, 26624], P('gx', 'gy'), may hold values from -0.0625 to 0.0625
- gate_scale: float32 [26624], P('gy'), may hold values from 0.3 to 3
- up_scale: float32 [26624], P('gy'), may hold values from 0.3 to 3
- down_weight: bfloat16 [26624, 8192], P('gy', 'gx'), may hold values from -0.0390625 to 0.0390625
- down_scale: float32 [8192], P('gx'), may hold values from 0.3 to 3
Outputs:
- mixed: bfloat16 [2, 384, 8192], P(None, ('groups', 'gy'), 'gx'), parts along dimension 1
The draws below stay inside these ranges and needn't reach their ends.
There are 2 independent parts, one for each index of `groups`. The reference program is written for one: setup_inputs(seed, part) draws one part's arguments, and reference() takes and returns one part's arrays. A program takes and returns all parts, laid end to end along the dimension named above; an argument that names none is the same for every part. Nothing has to cross between parts.
All inputs are finite; a program needn't handle non-finite values.
Results may differ from the reference program's by a relative error of at most 0.028.
Values may be sent and summed in bfloat16 or wider, within the bound.
No kernel may reach another device: no remote copies, remote signals or barrier semaphores. Data moves between devices by JAX's collectives and lax.ppermute only.
A program may use at most 256 MiB of HBM per device.

```python
import math
import jax
import jax.numpy as jnp
from jax import lax

D = 8192
FF = 26624
ROWS = 192
STEPS = 2
N_GX = 4
N_GY = 4


def steps_of(own_key, dims, split, smallest, largest):
    factor_of, own = 1.0, jax.random.fold_in(own_key, 6)
    for dim, shards_of in split:
        draws = jnp.exp(jax.random.uniform(jax.random.fold_in(own, dim), (shards_of,), jnp.float32, smallest / len(split), largest / len(split)))
        factor_of = factor_of * jnp.repeat(draws, dims[dim] // shards_of).reshape([-1 if axis == dim else 1 for axis in range(len(dims))])
    return factor_of


def normal_values(stream_key, shape, scale, bound, cuts=(), dtype=jnp.bfloat16):
    array = jax.random.normal(stream_key, shape, jnp.float32) * scale
    if len(cuts) > 0:
        array = steps_of(stream_key, shape, cuts, -0.22, 0.18) * array
    return jnp.clip(array, min=-bound, max=bound).astype(dtype)


def setup_inputs(seed: int = 0, part: int = 0) -> dict:
    key_of = jax.random.split(jax.random.key(seed), 8)
    part_keys = jax.random.split(jax.random.fold_in(key_of[7], part), 8)
    return {
        "tokens": normal_values(part_keys[0], (STEPS, ROWS, D), 1.0, 6.0, ((1, 4), (2, 4))),
        "gate_weight": normal_values(key_of[1], (D, FF), D ** -0.5, 0.0625, ((0, 4), (1, 4))),
        "up_weight": normal_values(key_of[2], (D, FF), D ** -0.5, 0.0625, ((0, 4), (1, 4))),
        "gate_scale": jnp.clip(jnp.exp(math.log(3.0) - 2.3025851 * jax.random.uniform(key_of[3], (FF,), jnp.float32) ** steps_of(key_of[3], (FF,), ((0, 4),), -0.2, 0.2)), 0.3, 3.0),
        "up_scale": jnp.clip(jnp.exp(math.log(3.0) - 2.3025851 * jax.random.uniform(key_of[4], (FF,), jnp.float32) ** steps_of(key_of[4], (FF,), ((0, 4),), -0.2, 0.2)), 0.3, 3.0),
        "down_weight": normal_values(key_of[5], (FF, D), FF ** -0.5, 0.0390625, ((0, 4), (1, 4))),
        "down_scale": jnp.clip(jnp.exp(math.log(3.0) - 2.3025851 * jax.random.uniform(key_of[6], (D,), jnp.float32) ** steps_of(key_of[6], (D,), ((0, 4),), -0.2, 0.2)), 0.3, 3.0),
    }


def rounded(value):
    return lax.optimization_barrier(value.astype(jnp.bfloat16)).astype(jnp.float32)


def reference(tokens, gate_weight, up_weight, gate_scale, up_scale, down_weight, down_scale):
    total_rows = STEPS * ROWS
    width_piece = D // N_GX
    hidden_piece = FF // N_GY
    pieces = tokens.reshape(total_rows, N_GX, width_piece).transpose(1, 0, 2)
    gate_pieces = gate_weight.reshape(N_GX, width_piece, FF)
    up_pieces = up_weight.reshape(N_GX, width_piece, FF)

    def add_width(carry, item):
        rows_in, gate_w, up_w = item
        gate_term = rounded(jnp.dot(rows_in, gate_w, preferred_element_type=jnp.float32))
        up_term = rounded(jnp.dot(rows_in, up_w, preferred_element_type=jnp.float32))
        return (carry[0] + gate_term, carry[1] + up_term), None

    start = jnp.zeros((total_rows, FF), jnp.float32)
    (gate_sum, up_sum), _ = lax.scan(add_width, (start, start), (pieces, gate_pieces, up_pieces))
    gate = gate_sum * gate_scale[None, :]
    up = up_sum * up_scale[None, :]
    hidden = (jax.nn.silu(gate) * up).astype(jnp.bfloat16)
    hidden_pieces = hidden.reshape(total_rows, N_GY, hidden_piece).transpose(1, 0, 2)
    down_pieces = down_weight.reshape(N_GY, hidden_piece, D)

    def add_hidden(carry, item):
        rows_in, down_w = item
        return carry + rounded(jnp.dot(rows_in, down_w, preferred_element_type=jnp.float32)), None

    down_sum, _ = lax.scan(add_hidden, jnp.zeros((total_rows, D), jnp.float32), (hidden_pieces, down_pieces))
    mixed = (down_sum * down_scale[None, :]).astype(jnp.bfloat16)
    return mixed.reshape(STEPS, ROWS, D)
```

```python
import functools

import jax
import jax.numpy as jnp
from jax import lax
from jax.experimental import pallas as pl
from jax.experimental.pallas import tpu as pltpu
from jax.sharding import PartitionSpec as P

VMEM = 48 * 1024 * 1024


def width_of(units):
    return max(w for w in range(128, 513, 128) if units % w == 0)


def tile_of(size, limit):
    return max(t for t in range(128, min(size, limit) + 1, 128) if size % t == 0)


def params(**more):
    return pltpu.CompilerParams(vmem_limit_bytes=VMEM, **more)


def project(place, rows, gate_weight, up_weight, step, width):
    count, depth = rows.shape
    chunks = gate_weight.shape[1] // width
    tile = tile_of(width, 256)
    tiles = width // tile

    def kernel(place_ref, rows_ref, gate_ref, up_ref, out_ref):
        x = rows_ref[...]
        out_ref[0] = jnp.dot(x, gate_ref[...], preferred_element_type=jnp.float32).astype(jnp.bfloat16)
        out_ref[1] = jnp.dot(x, up_ref[...], preferred_element_type=jnp.float32).astype(jnp.bfloat16)

    def weight(j, place_ref):
        return 0, jnp.clip(step - place_ref[0], 0, chunks - 1) * tiles + j

    return pl.pallas_call(
        kernel,
        grid_spec=pltpu.PrefetchScalarGridSpec(
            num_scalar_prefetch=1,
            grid=(tiles,),
            in_specs=[
                pl.BlockSpec((count, depth), lambda j, place_ref: (0, 0)),
                pl.BlockSpec((depth, tile), weight),
                pl.BlockSpec((depth, tile), weight),
            ],
            out_specs=pl.BlockSpec((2, count, tile), lambda j, place_ref: (0, 0, j)),
        ),
        out_shape=jax.ShapeDtypeStruct((2, count, width), jnp.bfloat16),
        compiler_params=params(),
        name="project",
    )(place, rows, gate_weight, up_weight)


def combine(place, part, received, scales, step, last):
    _, count, width = part.shape
    chunks = scales.shape[0]
    rows = count // 3 if count % 48 == 0 else count

    def kernel(place_ref, part_ref, recv_ref, scale_ref, sum_ref, hidden_ref):
        gate = part_ref[0].astype(jnp.float32) + recv_ref[0].astype(jnp.float32)
        up = part_ref[1].astype(jnp.float32) + recv_ref[1].astype(jnp.float32)

        @pl.when(place_ref[0] != last)
        def _():
            sum_ref[0] = gate.astype(jnp.bfloat16)
            sum_ref[1] = up.astype(jnp.bfloat16)

        @pl.when(place_ref[0] == last)
        def _():
            g = gate * scale_ref[0, 0:1, :]
            u = up * scale_ref[0, 1:2, :]
            hidden_ref[...] = (jax.nn.silu(g) * u).astype(jnp.bfloat16)

    def scale(i, place_ref):
        return jnp.clip(step - place_ref[0], 0, chunks - 1), 0, 0

    block = pl.BlockSpec((2, rows, width), lambda i, place_ref: (0, i, 0))
    return pl.pallas_call(
        kernel,
        grid_spec=pltpu.PrefetchScalarGridSpec(
            num_scalar_prefetch=1,
            grid=(count // rows,),
            in_specs=[block, block, pl.BlockSpec((1, 2, width), scale)],
            out_specs=[block, pl.BlockSpec((rows, width), lambda i, place_ref: (i, 0))],
        ),
        out_shape=[
            jax.ShapeDtypeStruct(part.shape, jnp.bfloat16),
            jax.ShapeDtypeStruct((count, width), jnp.bfloat16),
        ],
        compiler_params=params(),
        name="combine",
    )(place, part, received, scales)


def reduce_down(place, hidden, received, down_weight, total, step, last):
    count, width = hidden.shape
    outs = down_weight.shape[1]
    chunks = down_weight.shape[0] // width
    tile = tile_of(outs, 512)

    def kernel(place_ref, hidden_ref, recv_ref, weight_ref, *rest):
        total_ref = rest[0] if total is not None else None
        send_ref, out_ref = rest[-2:]

        @pl.when(pl.program_id(0) == 0)
        def _():
            @pl.when(place_ref[0] == last)
            def _():
                send_ref[...] = hidden_ref[...]

            @pl.when(place_ref[0] != last)
            def _():
                send_ref[...] = recv_ref[...]

        chunk = step - 2 * last + place_ref[0]
        valid = jnp.logical_and(chunk >= 0, chunk < chunks)

        @pl.when(valid)
        def _():
            term = jnp.dot(send_ref[...], weight_ref[...], preferred_element_type=jnp.float32)
            out_ref[...] = term if total_ref is None else total_ref[...] + term

        @pl.when(jnp.logical_not(valid))
        def _():
            out_ref[...] = jnp.zeros_like(out_ref) if total_ref is None else total_ref[...]

    def weight(j, place_ref):
        return jnp.clip(step - 2 * last + place_ref[0], 0, chunks - 1), j

    whole = pl.BlockSpec((count, width), lambda j, place_ref: (0, 0))
    part = pl.BlockSpec((count, tile), lambda j, place_ref: (0, j))
    more = [] if total is None else [total]
    return pl.pallas_call(
        kernel,
        grid_spec=pltpu.PrefetchScalarGridSpec(
            num_scalar_prefetch=1,
            grid=(outs // tile,),
            in_specs=[whole, whole, pl.BlockSpec((width, tile), weight)] + [part] * len(more),
            out_specs=[whole, part],
        ),
        out_shape=[
            jax.ShapeDtypeStruct((count, width), jnp.bfloat16),
            jax.ShapeDtypeStruct((count, outs), jnp.float32),
        ],
        input_output_aliases={4: 1} if more else {},
        compiler_params=params(),
        name="reduce_down",
    )(place, hidden, received, down_weight, *more)


def per_device(mesh, tokens, gate_weight, up_weight, gate_scale, up_scale, down_weight, down_scale):
    n_gx, n_gy = mesh.shape["gx"], mesh.shape["gy"]
    last = n_gx - 1
    towards, back = [], []
    for z in range(n_gx):
        for g in range(n_gy):
            to = z - 1 if g % 2 == 0 else z + 1
            if 0 <= to < n_gx:
                towards.append((z * n_gy + g, to * n_gy + g))
                back.append((to * n_gy + g, z * n_gy + g))
    z, g = lax.axis_index("gx"), lax.axis_index("gy")
    place = jnp.where(g % 2 == 0, last - z, z).astype(jnp.int32).reshape(1)

    units = gate_weight.shape[1]
    width = width_of(units)
    chunks = units // width
    scales = jnp.stack([gate_scale.reshape(chunks, width), up_scale.reshape(chunks, width)], axis=1)

    rows = lax.all_gather(tokens, "gy", axis=1, tiled=True)
    steps, count, depth = rows.shape
    rows = rows.reshape(steps * count, depth)

    send, hidden, total, passed = None, None, None, None
    for step in range(chunks + 2 * last):
        summing = step < chunks + last
        if summing:
            part = project(place, rows, gate_weight, up_weight, step, width)
            if step == 0:
                got = jnp.zeros_like(part)
            else:
                got = lax.ppermute(send, ("gx", "gy"), towards)
            send, hidden = combine(place, part, got, scales, step, last)
        if step >= last:
            if step == last:
                held = jnp.zeros_like(hidden)
            else:
                held = lax.ppermute(passed, ("gx", "gy"), back)
            passed, total = reduce_down(place, hidden, held, down_weight, total, step, last)

    down = total.astype(jnp.bfloat16).reshape(steps, count, -1)
    down_sum = lax.psum_scatter(down, "gy", scatter_dimension=1, tiled=True).astype(jnp.float32)
    return (down_sum * down_scale).astype(jnp.bfloat16)


def solution(mesh):
    placed = (
        P(None, ("groups", "gy"), "gx"),
        P("gx", "gy"),
        P("gx", "gy"),
        P("gy"),
        P("gy"),
        P("gy", "gx"),
        P("gx"),
    )
    return jax.shard_map(
        functools.partial(per_device, mesh),
        mesh=mesh,
        in_specs=placed,
        out_specs=P(None, ("groups", "gy"), "gx"),
        check_vma=False,
    )
```

```python
import functools

import jax
import jax.numpy as jnp
from jax import lax
from jax.experimental import pallas as pl
from jax.experimental.pallas import tpu as pltpu
from jax.sharding import PartitionSpec as P

LIMIT = 44 * 1024 * 1024
FLOPS = 5_000_000_000
TOKEN = jax.ShapeDtypeStruct((8, 128), jnp.float32)


def width_of(units):
    return max(w for w in range(128, 513, 128) if units % w == 0)


def tile_of(size, limit):
    return max(t for t in range(128, min(size, limit) + 1, 128) if size % t == 0)


def held_whole():
    return pl.BlockSpec(memory_space=pltpu.VMEM)


def call(kernel, name, in_specs, out_shape, operands, flops=1, aliases={}, scratch=()):
    return pl.pallas_call(
        kernel,
        grid_spec=pltpu.PrefetchScalarGridSpec(
            num_scalar_prefetch=1,
            grid=(1,),
            in_specs=in_specs,
            out_specs=[held_whole()] * len(out_shape),
            scratch_shapes=scratch,
        ),
        out_shape=out_shape,
        input_output_aliases=aliases,
        compiler_params=pltpu.CompilerParams(vmem_limit_bytes=LIMIT),
        cost_estimate=pl.CostEstimate(flops=flops, bytes_accessed=1, transcendentals=0),
        name=name,
    )(*operands)


def work(place, rows, gate_weight, up_weight, chunk, down_weight, total, after, step, width, parts, last):
    ups, downs = rows is not None, chunk is not None
    chunks = down_weight.shape[0] // width
    depth, outs = gate_weight.shape[0], down_weight.shape[1]
    piece = width // parts
    down_tile = tile_of(outs, 512)
    operands = [place, after]
    specs = [held_whole()]
    shapes, scratch, aliases = [TOKEN], [], {}
    if ups:
        count = rows.shape[0]
        operands += [rows, gate_weight, up_weight]
        specs += [held_whole()] + [pl.BlockSpec(memory_space=pltpu.HBM)] * 2
        shapes += [jax.ShapeDtypeStruct((2, count, piece), jnp.bfloat16)] * parts
        scratch += [pltpu.VMEM((parts, 2, depth, piece), jnp.bfloat16), pltpu.SemaphoreType.DMA((parts, 2))]
    if downs:
        operands += [chunk, down_weight, total]
        specs += [held_whole(), pl.BlockSpec(memory_space=pltpu.HBM), held_whole()]
        shapes += [jax.ShapeDtypeStruct(total.shape, jnp.float32)]
        aliases = {len(operands) - 1: len(shapes) - 1}
        tiles = outs // down_tile
        scratch += [pltpu.VMEM((tiles, width, down_tile), jnp.bfloat16), pltpu.SemaphoreType.DMA((tiles,))]

    def kernel(place_ref, after_ref, *refs):
        refs = list(refs)
        take = lambda number: [refs.pop(0) for _ in range(number)]
        rows_ref, gate_ref, up_ref = take(3) if ups else [None] * 3
        chunk_ref, down_ref, total_ref = take(3) if downs else [None] * 3
        (token_ref,) = take(1)
        part_refs = take(parts) if ups else []
        (out_ref,) = take(1) if downs else [None]
        up_buffer, up_sem = take(2) if ups else [None] * 2
        down_buffer, down_sem = take(2) if downs else [None] * 2
        token_ref[...] = jnp.zeros_like(token_ref)
        added = jnp.clip(step + 1 - place_ref[0], 0, chunks - 1)
        held = step - 2 * last + place_ref[0]
        row = pl.multiple_of(jnp.clip(held, 0, chunks - 1) * width, width)

        up_copies, down_copies = [], []
        if ups:
            for part in range(parts):
                column = pl.multiple_of(added * width + part * piece, piece)
                for which, weight_ref in enumerate([gate_ref, up_ref]):
                    up_copies.append(
                        pltpu.make_async_copy(
                            weight_ref.at[:, pl.ds(column, piece)],
                            up_buffer.at[part, which],
                            up_sem.at[part, which],
                        )
                    )
        if downs:
            for tile in range(tiles):
                down_copies.append(
                    pltpu.make_async_copy(
                        down_ref.at[pl.ds(row, width), tile * down_tile : (tile + 1) * down_tile],
                        down_buffer.at[tile],
                        down_sem.at[tile],
                    )
                )
        for copy in up_copies + down_copies:
            copy.start()
        if ups:
            for part in range(parts):
                for which in range(2):
                    up_copies[2 * part + which].wait()
                    part_refs[part][which] = jnp.dot(
                        rows_ref[...], up_buffer[part, which], preferred_element_type=jnp.float32
                    ).astype(jnp.bfloat16)
        if downs:
            inside = jnp.logical_and(held >= 0, held < chunks)
            for tile in range(tiles):
                down_copies[tile].wait()

                @pl.when(inside)
                def _():
                    columns = slice(tile * down_tile, (tile + 1) * down_tile)
                    term = jnp.dot(chunk_ref[...], down_buffer[tile], preferred_element_type=jnp.float32)
                    out_ref[:, columns] = total_ref[:, columns] + term

    result = list(call(kernel, "work", specs, shapes, operands, FLOPS, aliases, scratch))
    after = result.pop(0)
    pieces = [result.pop(0) for _ in range(parts)] if ups else None
    return pieces, result.pop(0) if downs else total, after


def combine(place, part, received, scales, after, step, index, last):
    _, count, piece = part.shape
    chunks = scales.shape[0]

    def kernel(place_ref, part_ref, recv_ref, scale_ref, after_ref, sum_ref, hidden_ref, token_ref):
        token_ref[...] = jnp.zeros_like(token_ref)

        @pl.when(place_ref[0] != last)
        def _():
            sum_ref[...] = (part_ref[...].astype(jnp.float32) + recv_ref[...].astype(jnp.float32)).astype(jnp.bfloat16)

        @pl.when(place_ref[0] == last)
        def _():
            gate = part_ref[0].astype(jnp.float32) + recv_ref[0].astype(jnp.float32)
            up = part_ref[1].astype(jnp.float32) + recv_ref[1].astype(jnp.float32)
            g = gate * scale_ref[0, 0:1, :]
            u = up * scale_ref[0, 1:2, :]
            hidden_ref[...] = (jax.nn.silu(g) * u).astype(jnp.bfloat16)

    def scale(i, place_ref):
        return jnp.clip(step - place_ref[0], 0, chunks - 1), 0, index

    return call(
        kernel,
        "combine",
        [held_whole(), held_whole(), pl.BlockSpec((1, 2, piece), scale), held_whole()],
        [
            jax.ShapeDtypeStruct(part.shape, jnp.bfloat16),
            jax.ShapeDtypeStruct((count, piece), jnp.bfloat16),
            TOKEN,
        ],
        (place, part, received, scales, after),
    )


def choose(place, pieces, received, after, last):
    count, width = received.shape
    piece = width // len(pieces)

    def kernel(place_ref, recv_ref, after_ref, *refs):
        pass_ref, token_ref = refs[-2:]
        token_ref[...] = jnp.zeros_like(token_ref)

        @pl.when(place_ref[0] == last)
        def _():
            for index, piece_ref in enumerate(refs[:-2]):
                pass_ref[:, index * piece : (index + 1) * piece] = piece_ref[...]

        @pl.when(place_ref[0] != last)
        def _():
            pass_ref[...] = recv_ref[...]

    return call(
        kernel,
        "choose",
        [held_whole()] * (2 + len(pieces)),
        [jax.ShapeDtypeStruct(received.shape, jnp.bfloat16), TOKEN],
        (place, received, after, *pieces),
    )


def swap(array, bit, size):
    return lax.ppermute(array, "gy", [(g, g ^ bit) for g in range(size)])


def gather(own, size):
    blocks, bit = [own], size // 2
    while bit >= 1:
        blocks = blocks + [swap(block, bit, size) for block in blocks]
        bit //= 2
    return jnp.concatenate(blocks, axis=0)


def scatter(total, size):
    bit = 1
    while bit < size:
        half = total.shape[0] // 2
        got = swap(total[half:].astype(jnp.bfloat16), bit, size)
        total = total[:half] + got.astype(jnp.float32)
        bit *= 2
    return total


def per_device(mesh, tokens, gate_weight, up_weight, gate_scale, up_scale, down_weight, down_scale):
    n_gx, n_gy = mesh.shape["gx"], mesh.shape["gy"]
    last = n_gx - 1
    towards, back = [], []
    for z in range(n_gx):
        for g in range(n_gy):
            to = z - 1 if g % 2 == 0 else z + 1
            if 0 <= to < n_gx:
                towards.append((z * n_gy + g, to * n_gy + g))
                back.append((to * n_gy + g, z * n_gy + g))
    z, g = lax.axis_index("gx"), lax.axis_index("gy")
    place = jnp.where(g % 2 == 0, last - z, z).astype(jnp.int32).reshape(1)

    units = gate_weight.shape[1]
    width = width_of(units)
    chunks = units // width
    scales = jnp.stack([gate_scale.reshape(chunks, width), up_scale.reshape(chunks, width)], axis=1)

    steps, own, depth = tokens.shape
    rows = gather(tokens.reshape(steps * own, depth), n_gy)
    count, outs = rows.shape[0], down_weight.shape[1]

    after = jnp.zeros(TOKEN.shape, TOKEN.dtype)
    parts = 2 if width % 256 == 0 else 1
    got = [jnp.zeros((2, count, width // parts), jnp.bfloat16)] * parts
    held = jnp.zeros((count, width), jnp.bfloat16)
    total = jnp.zeros((count, outs), jnp.float32)
    summing = chunks + last
    both = functools.partial(work, width=width, parts=parts, last=last)
    part, _, after = both(place, rows, gate_weight, up_weight, None, down_weight, None, after, -1)
    for step in range(chunks + 2 * last):
        chunk, pieces = None, [None] * parts
        if step < summing:
            for index in range(parts):
                send, pieces[index], after = combine(
                    place, part[index], got[index], scales, after, step, index, last
                )
                if step + 1 < summing:
                    got[index] = lax.ppermute(send, ("gx", "gy"), towards)
        if step >= last:
            chunk = held
            if step < summing:
                chunk, after = choose(place, pieces, held, after, last)
            held = lax.ppermute(chunk, ("gx", "gy"), back)
        part, total, after = both(
            place,
            rows if step + 1 < summing else None,
            gate_weight,
            up_weight,
            chunk,
            down_weight,
            total,
            after,
            step,
        )

    mixed = scatter(total, n_gy).reshape(steps, own, outs) * down_scale
    return mixed.astype(jnp.bfloat16)


def solution(mesh):
    placed = (
        P(None, ("groups", "gy"), "gx"),
        P("gx", "gy"),
        P("gx", "gy"),
        P("gy"),
        P("gy"),
        P("gy", "gx"),
        P("gx"),
    )
    return jax.shard_map(
        functools.partial(per_device, mesh),
        mesh=mesh,
        in_specs=placed,
        out_specs=P(None, ("groups", "gy"), "gx"),
        check_vma=False,
    )
```

```python
import functools

import jax
import jax.numpy as jnp
from jax import lax
from jax.experimental import pallas as pl
from jax.experimental.pallas import tpu as pltpu
from jax.sharding import PartitionSpec as P

LIMIT = 24 * 1024 * 1024
FLOPS = 5_000_000_000
TOKEN = jax.ShapeDtypeStruct((8, 128), jnp.float32)


def width_of(units):
    return max(w for w in range(128, 513, 128) if units % w == 0)


def tile_of(size, limit):
    return max(t for t in range(128, min(size, limit) + 1, 128) if size % t == 0)


def held_whole():
    return pl.BlockSpec(memory_space=pltpu.VMEM)


def call(kernel, name, in_specs, out_shape, operands, flops=1, aliases={}, scratch=()):
    return pl.pallas_call(
        kernel,
        in_specs=[pl.BlockSpec(memory_space=pltpu.SMEM)] + in_specs,
        out_specs=[held_whole()] * len(out_shape),
        scratch_shapes=scratch,
        out_shape=out_shape,
        input_output_aliases=aliases,
        compiler_params=pltpu.CompilerParams(vmem_limit_bytes=LIMIT),
        cost_estimate=pl.CostEstimate(flops=flops, bytes_accessed=1, transcendentals=0),
        name=name,
    )(*operands)


def work(place, after, step, width, parts, last, gate_weight, up_weight, down_weight, ups, downs, load_ups, load_downs):
    chunks = down_weight.shape[0] // width
    depth, outs = gate_weight.shape[0], down_weight.shape[1]
    piece = width // parts
    operands, specs = [place, after], [held_whole()]
    shapes, scratch, aliases = [TOKEN], [], {}
    if ups:
        operands += ups
        specs += [held_whole()] * 2
        shapes += [jax.ShapeDtypeStruct((2, ups[0].shape[0], piece), jnp.bfloat16)] * parts
    if downs:
        operands += downs
        specs += [held_whole()] * 3
        shapes += [jax.ShapeDtypeStruct(downs[2].shape, jnp.float32)]
        aliases = {len(operands) - 1: len(shapes) - 1}
    loads = []
    if load_ups:
        loads += [gate_weight, up_weight]
        shapes += [jax.ShapeDtypeStruct((2, depth, width), jnp.bfloat16)]
    if load_downs:
        loads += [down_weight]
        shapes += [jax.ShapeDtypeStruct((width, outs), jnp.bfloat16)]
    operands += loads
    specs += [pl.BlockSpec(memory_space=pltpu.HBM)] * len(loads)
    if loads:
        scratch = [pltpu.SemaphoreType.DMA((len(loads),))]

    def kernel(place_ref, after_ref, *refs):
        refs = list(refs)
        take = lambda number: [refs.pop(0) for _ in range(number)]
        rows_ref, up_ref = take(2) if ups else [None] * 2
        chunk_ref, down_ref, total_ref = take(3) if downs else [None] * 3
        load_refs = take(len(loads))
        (token_ref,) = take(1)
        part_refs = take(parts) if ups else []
        (out_ref,) = take(1) if downs else [None]
        (next_up,) = take(1) if load_ups else [None]
        (next_down,) = take(1) if load_downs else [None]
        added = jnp.clip(step + 2 - place_ref[0], 0, chunks - 1)
        held = step - 2 * last + place_ref[0]
        kept = jnp.clip(held + 1, 0, chunks - 1)
        pairs = []
        if load_ups:
            columns = pl.ds(pl.multiple_of(added * width, width), width)
            pairs += [(ref.at[:, columns], next_up.at[which]) for which, ref in enumerate(load_refs[:2])]
        if load_downs:
            pairs += [(load_refs[-1].at[pl.ds(pl.multiple_of(kept * width, width), width)], next_down)]
        copies = [pltpu.make_async_copy(*pair, refs[0].at[index]) for index, pair in enumerate(pairs)]
        for copy in copies:
            copy.start()
        token_ref[...] = jnp.zeros_like(token_ref)
        if ups:
            for part in range(parts):
                for which in range(2):
                    part_refs[part][which] = jnp.dot(
                        rows_ref[...],
                        up_ref[which, :, part * piece : (part + 1) * piece],
                        preferred_element_type=jnp.float32,
                    ).astype(jnp.bfloat16)
        if downs:

            @pl.when(jnp.logical_and(held >= 0, held < chunks))
            def _():
                term = jnp.dot(chunk_ref[...], down_ref[...], preferred_element_type=jnp.float32)
                out_ref[...] = total_ref[...] + term

        for copy in copies:
            copy.wait()

    flops = FLOPS if ups or downs else 1
    result = list(call(kernel, "work" if ups or downs else "load", specs, shapes, operands, flops, aliases, scratch))
    after = result.pop(0)
    pieces = [result.pop(0) for _ in range(parts)] if ups else None
    total = result.pop(0) if downs else None
    next_up = result.pop(0) if load_ups else None
    return after, pieces, total, next_up, result.pop(0) if load_downs else None


def combine(place, part, received, scales, after, step, index, last):
    _, count, piece = part.shape
    chunks = scales.shape[0]

    def kernel(place_ref, part_ref, recv_ref, scale_ref, after_ref, sum_ref, hidden_ref, token_ref):
        token_ref[...] = jnp.zeros_like(token_ref)

        @pl.when(place_ref[0] != last)
        def _():
            sum_ref[...] = (part_ref[...].astype(jnp.float32) + recv_ref[...].astype(jnp.float32)).astype(jnp.bfloat16)

        @pl.when(place_ref[0] == last)
        def _():
            gate = part_ref[0].astype(jnp.float32) + recv_ref[0].astype(jnp.float32)
            up = part_ref[1].astype(jnp.float32) + recv_ref[1].astype(jnp.float32)
            chunk = min(max(step - last, 0), chunks - 1)
            columns = slice(index * piece, (index + 1) * piece)
            g = gate * scale_ref[chunk, 0:1, columns]
            u = up * scale_ref[chunk, 1:2, columns]
            hidden_ref[...] = (jax.nn.silu(g) * u).astype(jnp.bfloat16)

    return call(
        kernel,
        "combine",
        [held_whole()] * 4,
        [
            jax.ShapeDtypeStruct(part.shape, jnp.bfloat16),
            jax.ShapeDtypeStruct((count, piece), jnp.bfloat16),
            TOKEN,
        ],
        (place, part, received, scales, after),
    )


def choose(place, pieces, received, after, last):
    count, width = received.shape
    piece = width // len(pieces)

    def kernel(place_ref, recv_ref, after_ref, *refs):
        pass_ref, token_ref = refs[-2:]
        token_ref[...] = jnp.zeros_like(token_ref)

        @pl.when(place_ref[0] == last)
        def _():
            for index, piece_ref in enumerate(refs[:-2]):
                pass_ref[:, index * piece : (index + 1) * piece] = piece_ref[...]

        @pl.when(place_ref[0] != last)
        def _():
            pass_ref[...] = recv_ref[...]

    return call(
        kernel,
        "choose",
        [held_whole()] * (2 + len(pieces)),
        [jax.ShapeDtypeStruct(received.shape, jnp.bfloat16), TOKEN],
        (place, received, after, *pieces),
    )


def swap(array, bit, size):
    return lax.ppermute(array, "gy", [(g, g ^ bit) for g in range(size)])


def gather(own, size):
    blocks, bit = [own], size // 2
    while bit >= 1:
        blocks = blocks + [swap(block, bit, size) for block in blocks]
        bit //= 2
    return jnp.concatenate(blocks, axis=0)


def scatter(total, size):
    bit = 1
    while bit < size:
        half = total.shape[0] // 2
        got = swap(total[half:].astype(jnp.bfloat16), bit, size)
        total = total[:half] + got.astype(jnp.float32)
        bit *= 2
    return total


def per_device(mesh, tokens, gate_weight, up_weight, gate_scale, up_scale, down_weight, down_scale):
    n_gx, n_gy = mesh.shape["gx"], mesh.shape["gy"]
    last = n_gx - 1
    towards, back = [], []
    for z in range(n_gx):
        for g in range(n_gy):
            to = z - 1 if g % 2 == 0 else z + 1
            if 0 <= to < n_gx:
                towards.append((z * n_gy + g, to * n_gy + g))
                back.append((to * n_gy + g, z * n_gy + g))
    z, g = lax.axis_index("gx"), lax.axis_index("gy")
    place = jnp.where(g % 2 == 0, last - z, z).astype(jnp.int32).reshape(1)

    units = gate_weight.shape[1]
    width = width_of(units)
    chunks = units // width
    scales = jnp.stack([gate_scale.reshape(chunks, width), up_scale.reshape(chunks, width)], axis=1)

    summing, ending = chunks + last, chunks + 2 * last
    parts = 2 if width % 256 == 0 else 1

    def run(after, step, ups, downs):
        return work(
            place, after, step, width, parts, last, gate_weight, up_weight, down_weight, ups, downs,
            step + 2 < summing, last <= step + 1 < ending,
        )

    after = jnp.zeros(TOKEN.shape, TOKEN.dtype)
    after, _, _, up_next, _ = run(after, -2, None, None)

    steps, own, depth = tokens.shape
    rows = gather(tokens.reshape(steps * own, depth), n_gy)
    count, outs = rows.shape[0], down_weight.shape[1]

    got = [jnp.zeros((2, count, width // parts), jnp.bfloat16)] * parts
    held = jnp.zeros((count, width), jnp.bfloat16)
    total = jnp.zeros((count, outs), jnp.float32)
    after, part, _, up_next, down_next = run(after, -1, [rows, up_next], None)
    for step in range(ending):
        pieces = [None] * parts
        ups, downs = None, None
        if step < summing:
            for index in range(parts):
                send, pieces[index], after = combine(
                    place, part[index], got[index], scales, after, step, index, last
                )
                if step + 1 < summing:
                    got[index] = lax.ppermute(send, ("gx", "gy"), towards)
                    ups = [rows, up_next]
        if step >= last:
            chunk = held
            if step < summing:
                chunk, after = choose(place, pieces, held, after, last)
            held = lax.ppermute(chunk, ("gx", "gy"), back)
            downs = [chunk, down_next, total]
        after, part, result, up_next, down_next = run(after, step, ups, downs)
        total = total if result is None else result

    mixed = scatter(total, n_gy).reshape(steps, own, outs) * down_scale
    return mixed.astype(jnp.bfloat16)


def solution(mesh):
    placed = (
        P(None, ("groups", "gy"), "gx"),
        P("gx", "gy"),
        P("gx", "gy"),
        P("gy"),
        P("gy"),
        P("gy", "gx"),
        P("gx"),
    )
    return jax.shard_map(
        functools.partial(per_device, mesh),
        mesh=mesh,
        in_specs=placed,
        out_specs=P(None, ("groups", "gy"), "gx"),
        check_vma=False,
    )
```

```python
import functools

import jax
import jax.numpy as jnp
from jax import lax
from jax.experimental import pallas as pl
from jax.experimental.pallas import tpu as pltpu
from jax.sharding import PartitionSpec as P

LIMIT = 28 * 1024 * 1024
FLOPS = 5_000_000_000
TOKEN = jax.ShapeDtypeStruct((8, 128), jnp.float32)


def width_of(units):
    return max(w for w in range(128, 513, 128) if units % w == 0)


def tile_of(size, limit):
    return max(t for t in range(128, min(size, limit) + 1, 128) if size % t == 0)


def held_whole():
    return pl.BlockSpec(memory_space=pltpu.VMEM)


def call(kernel, name, in_specs, out_shape, operands, flops=1, aliases={}, scratch=()):
    return pl.pallas_call(
        kernel,
        in_specs=[pl.BlockSpec(memory_space=pltpu.SMEM)] + in_specs,
        out_specs=[held_whole()] * len(out_shape),
        scratch_shapes=scratch,
        out_shape=out_shape,
        input_output_aliases=aliases,
        compiler_params=pltpu.CompilerParams(vmem_limit_bytes=LIMIT),
        cost_estimate=pl.CostEstimate(flops=flops, bytes_accessed=1, transcendentals=0),
        name=name,
    )(*operands)


def first(place, blocks, gate_weight, up_weight, width, parts):
    size, depth = blocks[0].shape
    count = size * len(blocks)
    chunks = gate_weight.shape[1] // width
    piece = width // parts

    def kernel(place_ref, *refs):
        block_refs, refs = refs[: len(blocks)], refs[len(blocks) :]
        weight_refs, (token_ref, rows_ref, *part_refs) = refs[:2], refs[2 : 4 + parts]
        next_up, buffer, sem, next_sem = refs[4 + parts :]
        added = jnp.clip(1 - place_ref[0], 0, chunks - 1)
        columns = pl.ds(pl.multiple_of(added * width, width), width)
        own, following = [], []
        for which, ref in enumerate(weight_refs):
            own.append(pltpu.make_async_copy(ref.at[:, 0:width], buffer.at[which], sem.at[which]))
            following.append(pltpu.make_async_copy(ref.at[:, columns], next_up.at[which], next_sem.at[which]))
        for copy in own + following:
            copy.start()
        token_ref[...] = jnp.zeros_like(token_ref)
        for index, block_ref in enumerate(block_refs):
            rows_ref[index * size : (index + 1) * size, :] = block_ref[...]
        for copy in own:
            copy.wait()
        project(rows_ref, buffer, part_refs, piece)
        for copy in following:
            copy.wait()

    after, rows, *result = call(
        kernel,
        "first",
        [held_whole()] * len(blocks) + [pl.BlockSpec(memory_space=pltpu.HBM)] * 2,
        [TOKEN, jax.ShapeDtypeStruct((count, depth), jnp.bfloat16)]
        + [jax.ShapeDtypeStruct((2, count, piece), jnp.bfloat16)] * parts
        + [jax.ShapeDtypeStruct((2, depth, width), jnp.bfloat16)],
        (place, *blocks, gate_weight, up_weight),
        scratch=[pltpu.VMEM((2, depth, width), jnp.bfloat16)] + [pltpu.SemaphoreType.DMA((2,))] * 2,
    )
    return after, rows, result[:-1], result[-1]


def project(rows_ref, up_ref, part_refs, piece):
    for part, part_ref in enumerate(part_refs):
        for which in range(2):
            part_ref[which] = jnp.dot(
                rows_ref[...],
                up_ref[which, :, part * piece : (part + 1) * piece],
                preferred_element_type=jnp.float32,
            ).astype(jnp.bfloat16)


def work(place, after, step, width, parts, last, gate_weight, up_weight, down_weight, ups, downs, load_ups, load_downs):
    chunks = down_weight.shape[0] // width
    depth, outs = gate_weight.shape[0], down_weight.shape[1]
    piece = width // parts
    operands, specs = [place, after], [held_whole()]
    shapes, scratch, aliases = [TOKEN], [], {}
    if ups:
        operands += ups
        specs += [held_whole()] * 2
        shapes += [jax.ShapeDtypeStruct((2, ups[0].shape[0], piece), jnp.bfloat16)] * parts
    held_chunk, down, totals = downs if downs else ([], None, [])
    if downs:
        operands += [*held_chunk, down, *totals]
        specs += [held_whole()] * (len(held_chunk) + 1 + len(totals))
        for index, total in enumerate(totals):
            aliases[len(operands) - len(totals) + index] = len(shapes)
            shapes += [jax.ShapeDtypeStruct(total.shape, jnp.float32)]
    loads = []
    if load_ups:
        loads += [gate_weight, up_weight]
        shapes += [jax.ShapeDtypeStruct((2, depth, width), jnp.bfloat16)]
    if load_downs:
        loads += [down_weight]
        shapes += [jax.ShapeDtypeStruct((width, outs), jnp.bfloat16)]
    operands += loads
    specs += [pl.BlockSpec(memory_space=pltpu.HBM)] * len(loads)
    if loads:
        scratch = [pltpu.SemaphoreType.DMA((len(loads),))]

    def kernel(place_ref, after_ref, *refs):
        refs = list(refs)
        take = lambda number: [refs.pop(0) for _ in range(number)]
        rows_ref, up_ref = take(2) if ups else [None] * 2
        chunk_refs = take(len(held_chunk))
        (down_ref,) = take(1) if downs else [None]
        total_refs = take(len(totals))
        load_refs = take(len(loads))
        (token_ref,) = take(1)
        part_refs = take(parts) if ups else []
        out_refs = take(len(totals))
        (next_up,) = take(1) if load_ups else [None]
        (next_down,) = take(1) if load_downs else [None]
        added = jnp.clip(step + 2 - place_ref[0], 0, chunks - 1)
        held = step - 2 * last + place_ref[0]
        kept = jnp.clip(held + 1, 0, chunks - 1)
        pairs = []
        if load_ups:
            columns = pl.ds(pl.multiple_of(added * width, width), width)
            pairs += [(ref.at[:, columns], next_up.at[which]) for which, ref in enumerate(load_refs[:2])]
        if load_downs:
            pairs += [(load_refs[-1].at[pl.ds(pl.multiple_of(kept * width, width), width)], next_down)]
        copies = [pltpu.make_async_copy(*pair, refs[0].at[index]) for index, pair in enumerate(pairs)]
        for copy in copies:
            copy.start()
        token_ref[...] = jnp.zeros_like(token_ref)
        if ups:
            project(rows_ref, up_ref, part_refs, piece)
        if downs:

            @pl.when(jnp.logical_and(held >= 0, held < chunks))
            def _():
                terms = [jnp.dot(ref[...], down_ref[...], preferred_element_type=jnp.float32) for ref in chunk_refs]
                if len(terms) < len(totals):
                    terms = jnp.split(terms[0], len(totals))
                for out_ref, total_ref, term in zip(out_refs, total_refs, terms):
                    out_ref[...] = total_ref[...] + term

        for copy in copies:
            copy.wait()

    result = list(call(kernel, "work", specs, shapes, operands, FLOPS if ups else 1, aliases, scratch))
    after = result.pop(0)
    pieces = [result.pop(0) for _ in range(parts)] if ups else None
    totals = [result.pop(0) for _ in totals]
    next_up = result.pop(0) if load_ups else None
    return after, pieces, totals, next_up, result.pop(0) if load_downs else None


def combine(place, part, received, scales, after, step, index, last, sends, acts):
    _, count, piece = part.shape
    chunks = scales.shape[0]
    shapes = [TOKEN]
    if sends:
        shapes += [jax.ShapeDtypeStruct(part.shape, jnp.bfloat16)]
    if acts:
        shapes += [jax.ShapeDtypeStruct((count, piece), jnp.bfloat16)]

    def kernel(place_ref, part_ref, recv_ref, scale_ref, after_ref, token_ref, *refs):
        token_ref[...] = jnp.zeros_like(token_ref)
        sum_ref, hidden_ref = refs[0], refs[-1]

        if sends:

            @pl.when(place_ref[0] != last)
            def _():
                total = part_ref[...].astype(jnp.float32) + recv_ref[...].astype(jnp.float32)
                sum_ref[...] = total.astype(jnp.bfloat16)

        if acts:

            @pl.when(place_ref[0] == last)
            def _():
                chunk = min(max(step - last, 0), chunks - 1)
                columns = slice(index * piece, (index + 1) * piece)
                gate = part_ref[0].astype(jnp.float32) + recv_ref[0].astype(jnp.float32)
                up = part_ref[1].astype(jnp.float32) + recv_ref[1].astype(jnp.float32)
                g = gate * scale_ref[chunk, 0:1, columns]
                u = up * scale_ref[chunk, 1:2, columns]
                hidden_ref[...] = (jax.nn.silu(g) * u).astype(jnp.bfloat16)

    after, *result = call(
        kernel, "combine", [held_whole()] * 4, shapes, (place, part, received, scales, after)
    )
    return after, result[0] if sends else None, result[-1] if acts else None


def choose(place, pieces, received, after, last, cuts):
    count, width = received.shape
    piece = width // len(pieces)
    size = count // cuts

    def kernel(place_ref, recv_ref, after_ref, *refs):
        token_ref, *pass_refs = refs[len(pieces) :]
        token_ref[...] = jnp.zeros_like(token_ref)

        @pl.when(place_ref[0] == last)
        def _():
            for cut, pass_ref in enumerate(pass_refs):
                for index, piece_ref in enumerate(refs[: len(pieces)]):
                    pass_ref[:, index * piece : (index + 1) * piece] = piece_ref[cut * size : (cut + 1) * size, :]

        @pl.when(place_ref[0] != last)
        def _():
            for cut, pass_ref in enumerate(pass_refs):
                pass_ref[...] = recv_ref[cut * size : (cut + 1) * size, :]

    after, *chunk = call(
        kernel,
        "choose",
        [held_whole()] * (2 + len(pieces)),
        [TOKEN] + [jax.ShapeDtypeStruct((size, width), jnp.bfloat16)] * cuts,
        (place, received, after, *pieces),
    )
    return after, chunk


def swap(array, bit, size):
    return lax.ppermute(array, "gy", [(g, g ^ bit) for g in range(size)])


def gather(own, size):
    blocks = [own]
    for i in range(1, size):
        blocks.append(swap(blocks[i & (i - 1)], i & -i, size))
    return blocks


def scatter(total, blocks, size):
    bit = 1
    while bit < blocks:
        pairs = total.reshape(blocks // bit // 2, 2, -1, total.shape[-1])
        got = swap(pairs[:, 1].astype(jnp.bfloat16), bit, size)
        total = pairs[:, 0] + got.astype(jnp.float32)
        bit *= 2
    return total.reshape(-1, total.shape[-1])


def per_device(mesh, tokens, gate_weight, up_weight, gate_scale, up_scale, down_weight, down_scale):
    n_gx, n_gy = mesh.shape["gx"], mesh.shape["gy"]
    last = n_gx - 1
    towards, back = [], []
    for z in range(n_gx):
        for g in range(n_gy):
            to = z - 1 if g % 2 == 0 else z + 1
            if 0 <= to < n_gx:
                towards.append((z * n_gy + g, to * n_gy + g))
                back.append((to * n_gy + g, z * n_gy + g))
    z, g = lax.axis_index("gx"), lax.axis_index("gy")
    place = jnp.where(g % 2 == 0, last - z, z).astype(jnp.int32).reshape(1)

    units = gate_weight.shape[1]
    width = width_of(units)
    chunks = units // width
    scales = jnp.stack([gate_scale.reshape(chunks, width), up_scale.reshape(chunks, width)], axis=1)

    summing, ending = chunks + last, chunks + 2 * last
    parts = 2 if width % 256 == 0 else 1

    def run(after, step, ups, downs, loads=True):
        return work(
            place, after, step, width, parts, last, gate_weight, up_weight, down_weight, ups, downs,
            loads and step + 2 < summing, loads and last <= step + 1 < ending,
        )

    steps, own, depth = tokens.shape
    blocks = gather(tokens.reshape(steps * own, depth), n_gy)
    after, rows, part, up_next = first(place, blocks, gate_weight, up_weight, width, parts)
    count, outs = rows.shape[0], down_weight.shape[1]

    totals = [jnp.zeros((count // 2, outs), jnp.float32)] * 2
    got = [None] * parts
    held = [jnp.zeros((count, width), jnp.bfloat16)]
    down_next = None
    for step in range(ending):
        pieces = [None] * parts
        ups = None
        if step < summing:
            for index in range(parts):
                send = part[index]
                if step > 0:
                    after, send, pieces[index] = combine(
                        place, part[index], got[index], scales, after, step, index, last,
                        step + 1 < summing, step >= last,
                    )
                if step + 1 < summing:
                    got[index] = lax.ppermute(send, ("gx", "gy"), towards)
                    ups = [rows, up_next]
        if step < last:
            after, part, _, up_next, down_next = run(after, step, ups, None)
            continue
        chunk = held
        if step < summing:
            after, chunk = choose(place, pieces, held[0], after, last, 1 if step + 1 < summing else 2)
        if step + 1 < ending:
            held = [None] * len(chunk)
            for half in reversed(range(len(chunk))):
                held[half] = lax.ppermute(chunk[half], ("gx", "gy"), back)
        if step < summing:
            after, part, totals, up_next, down_next = run(after, step, ups, [chunk, down_next, totals])
        else:
            after, _, far, _, _ = run(after, step, None, [chunk[1:], down_next, totals[1:]], False)
            after, _, near, _, down_next = run(after, step, None, [chunk[:1], down_next, totals[:1]])
            totals = near + far

    far = scatter(totals[1], n_gy // 2, n_gy)
    got = swap(far.astype(jnp.bfloat16), n_gy // 2, n_gy)
    near = scatter(totals[0], n_gy // 2, n_gy)
    mixed = (near + got.astype(jnp.float32)).reshape(steps, own, outs) * down_scale
    return mixed.astype(jnp.bfloat16)


def solution(mesh):
    placed = (
        P(None, ("groups", "gy"), "gx"),
        P("gx", "gy"),
        P("gx", "gy"),
        P("gy"),
        P("gy"),
        P("gy", "gx"),
        P("gx"),
    )
    return jax.shard_map(
        functools.partial(per_device, mesh),
        mesh=mesh,
        in_specs=placed,
        out_specs=P(None, ("groups", "gy"), "gx"),
        check_vma=False,
    )
```

```python
import functools

import jax
import jax.numpy as jnp
from jax import lax
from jax.experimental import pallas as pl
from jax.experimental.pallas import tpu as pltpu
from jax.sharding import PartitionSpec as P

LIMIT = 28 * 1024 * 1024
FLOPS = 5_000_000_000
TOKEN = jax.ShapeDtypeStruct((8, 128), jnp.float32)


def width_of(units):
    return max(w for w in range(128, 513, 128) if units % w == 0)


def tile_of(size, limit):
    return max(t for t in range(128, min(size, limit) + 1, 128) if size % t == 0)


def held_whole():
    return pl.BlockSpec(memory_space=pltpu.VMEM)


def call(kernel, name, in_specs, out_shape, operands, flops=1, aliases={}, scratch=()):
    return pl.pallas_call(
        kernel,
        in_specs=[pl.BlockSpec(memory_space=pltpu.SMEM)] + in_specs,
        out_specs=[held_whole()] * len(out_shape),
        scratch_shapes=scratch,
        out_shape=out_shape,
        input_output_aliases=aliases,
        compiler_params=pltpu.CompilerParams(vmem_limit_bytes=LIMIT),
        cost_estimate=pl.CostEstimate(flops=flops, bytes_accessed=1, transcendentals=0),
        name=name,
    )(*operands)


def first(place, blocks, gate_weight, up_weight, width, parts):
    size, depth = blocks[0].shape
    count = size * len(blocks)
    chunks = gate_weight.shape[1] // width
    piece = width // parts

    def kernel(place_ref, *refs):
        block_refs, refs = refs[: len(blocks)], refs[len(blocks) :]
        weight_refs, (token_ref, rows_ref, *part_refs) = refs[:2], refs[2 : 4 + parts]
        up_now, up_next, sem, next_sem = refs[4 + parts :]
        added = jnp.clip(1 - place_ref[0], 0, chunks - 1)
        columns = pl.ds(pl.multiple_of(added * width, width), width)
        own, following = [], []
        for which, ref in enumerate(weight_refs):
            own.append(pltpu.make_async_copy(ref.at[:, 0:width], up_now.at[which], sem.at[which]))
            following.append(pltpu.make_async_copy(ref.at[:, columns], up_next.at[which], next_sem.at[which]))
        for copy in own + following:
            copy.start()
        token_ref[...] = jnp.zeros_like(token_ref)
        for index, block_ref in enumerate(block_refs):
            rows_ref[index * size : (index + 1) * size, :] = block_ref[...]
        for copy in own:
            copy.wait()
        project(rows_ref, up_now, part_refs, piece)
        for copy in following:
            copy.wait()

    after, rows, *result = call(
        kernel,
        "first",
        [held_whole()] * len(blocks) + [pl.BlockSpec(memory_space=pltpu.HBM)] * 2,
        [TOKEN, jax.ShapeDtypeStruct((count, depth), jnp.bfloat16)]
        + [jax.ShapeDtypeStruct((2, count, piece), jnp.bfloat16)] * parts
        + [jax.ShapeDtypeStruct((2, depth, width), jnp.bfloat16)] * 2,
        (place, *blocks, gate_weight, up_weight),
        FLOPS,
        scratch=[pltpu.SemaphoreType.DMA((2,))] * 2,
    )
    return after, rows, result[:parts], result[parts], result[parts + 1]


def second(place, rows, blocks, part, up_now, after):
    half, depth = rows.shape
    size = blocks[0].shape[0]
    piece = part[0].shape[-1]
    count = half + size * len(blocks)

    def kernel(place_ref, after_ref, near_ref, up_ref, *refs):
        near_parts, refs = refs[: len(part)], refs[len(part) :]
        block_refs, (token_ref, rows_ref, *part_refs) = refs[: len(blocks)], refs[len(blocks) :]
        token_ref[...] = jnp.zeros_like(token_ref)
        for index, block_ref in enumerate(block_refs):
            rows_ref[half + index * size : half + (index + 1) * size, :] = block_ref[...]
        far_ref = rows_ref.at[half:count]
        project(far_ref, up_ref, [ref.at[:, half:count] for ref in part_refs], piece)
        rows_ref[0:half, :] = near_ref[...]
        for near_part, part_ref in zip(near_parts, part_refs):
            part_ref[:, 0:half, :] = near_part[...]

    after, rows, *result = call(
        kernel,
        "second",
        [held_whole()] * (3 + len(part) + len(blocks)),
        [TOKEN, jax.ShapeDtypeStruct((count, depth), jnp.bfloat16)]
        + [jax.ShapeDtypeStruct((2, count, piece), jnp.bfloat16)] * len(part),
        (place, after, rows, up_now, *part, *blocks),
    )
    return after, rows, result


def project(rows_ref, up_ref, part_refs, piece):
    for part, part_ref in enumerate(part_refs):
        for which in range(2):
            part_ref[which] = jnp.dot(
                rows_ref[...],
                up_ref[which, :, part * piece : (part + 1) * piece],
                preferred_element_type=jnp.float32,
            ).astype(jnp.bfloat16)


def work(place, after, step, width, parts, last, gate_weight, up_weight, down_weight, ups, downs, load_ups, load_downs):
    chunks = down_weight.shape[0] // width
    depth, outs = gate_weight.shape[0], down_weight.shape[1]
    piece = width // parts
    operands, specs = [place, after], [held_whole()]
    shapes, scratch, aliases = [TOKEN], [], {}
    if ups:
        operands += ups
        specs += [held_whole()] * 2
        shapes += [jax.ShapeDtypeStruct((2, ups[0].shape[0], piece), jnp.bfloat16)] * parts
    held_chunk, down, totals = downs if downs else ([], None, [])
    if downs:
        operands += [*held_chunk, down, *totals]
        specs += [held_whole()] * (len(held_chunk) + 1 + len(totals))
        for index, total in enumerate(totals):
            aliases[len(operands) - len(totals) + index] = len(shapes)
            shapes += [jax.ShapeDtypeStruct(total.shape, jnp.float32)]
    loads = []
    if load_ups:
        loads += [gate_weight, up_weight]
        shapes += [jax.ShapeDtypeStruct((2, depth, width), jnp.bfloat16)]
    if load_downs:
        loads += [down_weight]
        shapes += [jax.ShapeDtypeStruct((width, outs), jnp.bfloat16)]
    operands += loads
    specs += [pl.BlockSpec(memory_space=pltpu.HBM)] * len(loads)
    if loads:
        scratch = [pltpu.SemaphoreType.DMA((len(loads),))]

    def kernel(place_ref, after_ref, *refs):
        refs = list(refs)
        take = lambda number: [refs.pop(0) for _ in range(number)]
        rows_ref, up_ref = take(2) if ups else [None] * 2
        chunk_refs = take(len(held_chunk))
        (down_ref,) = take(1) if downs else [None]
        total_refs = take(len(totals))
        load_refs = take(len(loads))
        (token_ref,) = take(1)
        part_refs = take(parts) if ups else []
        out_refs = take(len(totals))
        (next_up,) = take(1) if load_ups else [None]
        (next_down,) = take(1) if load_downs else [None]
        added = jnp.clip(step + 2 - place_ref[0], 0, chunks - 1)
        held = step - 2 * last + place_ref[0]
        kept = jnp.clip(held + 1, 0, chunks - 1)
        pairs = []
        if load_ups:
            columns = pl.ds(pl.multiple_of(added * width, width), width)
            pairs += [(ref.at[:, columns], next_up.at[which]) for which, ref in enumerate(load_refs[:2])]
        if load_downs:
            pairs += [(load_refs[-1].at[pl.ds(pl.multiple_of(kept * width, width), width)], next_down)]
        copies = [pltpu.make_async_copy(*pair, refs[0].at[index]) for index, pair in enumerate(pairs)]
        for copy in copies:
            copy.start()
        token_ref[...] = jnp.zeros_like(token_ref)
        if ups:
            project(rows_ref, up_ref, part_refs, piece)
        if downs:

            @pl.when(jnp.logical_and(held >= 0, held < chunks))
            def _():
                terms = [jnp.dot(ref[...], down_ref[...], preferred_element_type=jnp.float32) for ref in chunk_refs]
                if len(terms) < len(totals):
                    terms = jnp.split(terms[0], len(totals))
                for out_ref, total_ref, term in zip(out_refs, total_refs, terms):
                    out_ref[...] = total_ref[...] + term

        for copy in copies:
            copy.wait()

    result = list(call(kernel, "work", specs, shapes, operands, FLOPS, aliases, scratch))
    after = result.pop(0)
    pieces = [result.pop(0) for _ in range(parts)] if ups else None
    totals = [result.pop(0) for _ in totals]
    next_up = result.pop(0) if load_ups else None
    return after, pieces, totals, next_up, result.pop(0) if load_downs else None


def combine(place, part, received, scales, after, step, index, last, sends, acts):
    _, count, piece = part.shape
    chunks = scales.shape[0]
    shapes = [TOKEN]
    if sends:
        shapes += [jax.ShapeDtypeStruct(part.shape, jnp.bfloat16)]
    if acts:
        shapes += [jax.ShapeDtypeStruct((count, piece), jnp.bfloat16)]

    def kernel(place_ref, part_ref, recv_ref, scale_ref, after_ref, token_ref, *refs):
        token_ref[...] = jnp.zeros_like(token_ref)
        sum_ref, hidden_ref = refs[0], refs[-1]

        if sends:

            @pl.when(place_ref[0] != last)
            def _():
                total = part_ref[...].astype(jnp.float32) + recv_ref[...].astype(jnp.float32)
                sum_ref[...] = total.astype(jnp.bfloat16)

        if acts:

            @pl.when(place_ref[0] == last)
            def _():
                chunk = min(max(step - last, 0), chunks - 1)
                columns = slice(index * piece, (index + 1) * piece)
                gate = part_ref[0].astype(jnp.float32) + recv_ref[0].astype(jnp.float32)
                up = part_ref[1].astype(jnp.float32) + recv_ref[1].astype(jnp.float32)
                g = gate * scale_ref[chunk, 0:1, columns]
                u = up * scale_ref[chunk, 1:2, columns]
                hidden_ref[...] = (jax.nn.silu(g) * u).astype(jnp.bfloat16)

    after, *result = call(
        kernel, "combine", [held_whole()] * 4, shapes, (place, part, received, scales, after)
    )
    return after, result[0] if sends else None, result[-1] if acts else None


def choose(place, pieces, received, after, last, cuts):
    count, width = received.shape
    piece = width // len(pieces)
    size = count // cuts

    def kernel(place_ref, recv_ref, after_ref, *refs):
        token_ref, *pass_refs = refs[len(pieces) :]
        token_ref[...] = jnp.zeros_like(token_ref)

        @pl.when(place_ref[0] == last)
        def _():
            for cut, pass_ref in enumerate(pass_refs):
                for index, piece_ref in enumerate(refs[: len(pieces)]):
                    pass_ref[:, index * piece : (index + 1) * piece] = piece_ref[cut * size : (cut + 1) * size, :]

        @pl.when(place_ref[0] != last)
        def _():
            for cut, pass_ref in enumerate(pass_refs):
                pass_ref[...] = recv_ref[cut * size : (cut + 1) * size, :]

    after, *chunk = call(
        kernel,
        "choose",
        [held_whole()] * (2 + len(pieces)),
        [TOKEN] + [jax.ShapeDtypeStruct((size, width), jnp.bfloat16)] * cuts,
        (place, received, after, *pieces),
    )
    return after, chunk


def swap(array, bit, size):
    return lax.ppermute(array, "gy", [(g, g ^ bit) for g in range(size)])


def gather(own, blocks, size):
    result = [own]
    for i in range(1, blocks):
        result.append(swap(result[i & (i - 1)], i & -i, size))
    return result


def scatter(total, blocks, size):
    bit = 1
    while bit < blocks:
        pairs = total.reshape(blocks // bit // 2, 2, -1, total.shape[-1])
        got = swap(pairs[:, 1].astype(jnp.bfloat16), bit, size)
        total = pairs[:, 0] + got.astype(jnp.float32)
        bit *= 2
    return total.reshape(-1, total.shape[-1])


def per_device(mesh, tokens, gate_weight, up_weight, gate_scale, up_scale, down_weight, down_scale):
    n_gx, n_gy = mesh.shape["gx"], mesh.shape["gy"]
    last = n_gx - 1
    towards, back = [], []
    for z in range(n_gx):
        for g in range(n_gy):
            to = z - 1 if g % 2 == 0 else z + 1
            if 0 <= to < n_gx:
                towards.append((z * n_gy + g, to * n_gy + g))
                back.append((to * n_gy + g, z * n_gy + g))
    z, g = lax.axis_index("gx"), lax.axis_index("gy")
    place = jnp.where(g % 2 == 0, last - z, z).astype(jnp.int32).reshape(1)

    units = gate_weight.shape[1]
    width = width_of(units)
    chunks = units // width
    scales = jnp.stack([gate_scale.reshape(chunks, width), up_scale.reshape(chunks, width)], axis=1)

    summing, ending = chunks + last, chunks + 2 * last
    parts = 2 if width % 256 == 0 else 1

    def run(after, step, ups, downs, loads=True):
        return work(
            place, after, step, width, parts, last, gate_weight, up_weight, down_weight, ups, downs,
            loads and step + 2 < summing, loads and last <= step + 1 < ending,
        )

    steps, own, depth = tokens.shape
    mine = tokens.reshape(steps * own, depth)
    far = gather(swap(mine, n_gy // 2, n_gy), n_gy // 2, n_gy)
    near = gather(mine, n_gy // 2, n_gy)
    after, rows, part, up_now, up_next = first(place, near, gate_weight, up_weight, width, parts)
    after, rows, part = second(place, rows, far, part, up_now, after)
    count, outs = rows.shape[0], down_weight.shape[1]

    totals = [jnp.zeros((count // 2, outs), jnp.float32)] * 2
    got = [None] * parts
    held = [jnp.zeros((count, width), jnp.bfloat16)]
    down_next = None
    for step in range(ending):
        pieces = [None] * parts
        ups = None
        if step < summing:
            for index in range(parts):
                send = part[index]
                if step > 0:
                    after, send, pieces[index] = combine(
                        place, part[index], got[index], scales, after, step, index, last,
                        step + 1 < summing, step >= last,
                    )
                if step + 1 < summing:
                    got[index] = lax.ppermute(send, ("gx", "gy"), towards)
                    ups = [rows, up_next]
        if step < last:
            after, part, _, up_next, down_next = run(after, step, ups, None)
            continue
        chunk = held
        if step < summing:
            after, chunk = choose(place, pieces, held[0], after, last, 1 if step + 1 < summing else 2)
        if step + 1 < ending:
            held = [None] * len(chunk)
            for half in reversed(range(len(chunk))):
                held[half] = lax.ppermute(chunk[half], ("gx", "gy"), back)
        if step < summing:
            after, part, totals, up_next, down_next = run(after, step, ups, [chunk, down_next, totals])
        else:
            after, _, far, _, _ = run(after, step, None, [chunk[1:], down_next, totals[1:]], False)
            after, _, near, _, down_next = run(after, step, None, [chunk[:1], down_next, totals[:1]])
            totals = near + far

    far = scatter(totals[1], n_gy // 2, n_gy)
    got = swap(far.astype(jnp.bfloat16), n_gy // 2, n_gy)
    near = scatter(totals[0], n_gy // 2, n_gy)
    mixed = (near + got.astype(jnp.float32)).reshape(steps, own, outs) * down_scale
    return mixed.astype(jnp.bfloat16)


def solution(mesh):
    placed = (
        P(None, ("groups", "gy"), "gx"),
        P("gx", "gy"),
        P("gx", "gy"),
        P("gy"),
        P("gy"),
        P("gy", "gx"),
        P("gx"),
    )
    return jax.shard_map(
        functools.partial(per_device, mesh),
        mesh=mesh,
        in_specs=placed,
        out_specs=P(None, ("groups", "gy"), "gx"),
        check_vma=False,
    )
```

```python
import functools

import jax
import jax.numpy as jnp
from jax import lax
from jax.experimental import pallas as pl
from jax.experimental.pallas import tpu as pltpu
from jax.sharding import PartitionSpec as P

LIMIT = 28 * 1024 * 1024
FLOPS = 5_000_000_000
TOKEN = jax.ShapeDtypeStruct((8, 128), jnp.float32)


def width_of(units):
    return max(w for w in range(128, 513, 128) if units % w == 0)


def tile_of(size, limit):
    return max(t for t in range(128, min(size, limit) + 1, 128) if size % t == 0)


def held_whole():
    return pl.BlockSpec(memory_space=pltpu.VMEM)


def call(kernel, name, in_specs, out_shape, operands, flops=1, aliases={}, scratch=()):
    return pl.pallas_call(
        kernel,
        in_specs=[pl.BlockSpec(memory_space=pltpu.SMEM)] + in_specs,
        out_specs=[held_whole()] * len(out_shape),
        scratch_shapes=scratch,
        out_shape=out_shape,
        input_output_aliases=aliases,
        compiler_params=pltpu.CompilerParams(vmem_limit_bytes=LIMIT),
        cost_estimate=pl.CostEstimate(flops=flops, bytes_accessed=1, transcendentals=0),
        name=name,
    )(*operands)


def first(place, blocks, gate_weight, up_weight, width, parts):
    size, depth = blocks[0].shape
    count = size * len(blocks)
    chunks = gate_weight.shape[1] // width
    piece = width // parts

    def kernel(place_ref, *refs):
        block_refs, refs = refs[: len(blocks)], refs[len(blocks) :]
        weight_refs, (token_ref, rows_ref, *part_refs) = refs[:2], refs[2 : 4 + parts]
        up_now, up_next, sem, next_sem = refs[4 + parts :]
        added = jnp.clip(1 - place_ref[0], 0, chunks - 1)
        columns = pl.ds(pl.multiple_of(added * width, width), width)
        own, following = [], []
        for which, ref in enumerate(weight_refs):
            own.append(pltpu.make_async_copy(ref.at[:, 0:width], up_now.at[which], sem.at[which]))
            following.append(pltpu.make_async_copy(ref.at[:, columns], up_next.at[which], next_sem.at[which]))
        for copy in own + following:
            copy.start()
        token_ref[...] = jnp.zeros_like(token_ref)
        for index, block_ref in enumerate(block_refs):
            rows_ref[index * size : (index + 1) * size, :] = block_ref[...]
        for copy in own:
            copy.wait()
        project(rows_ref, up_now, part_refs, piece)
        for copy in following:
            copy.wait()

    after, rows, *result = call(
        kernel,
        "first",
        [held_whole()] * len(blocks) + [pl.BlockSpec(memory_space=pltpu.HBM)] * 2,
        [TOKEN, jax.ShapeDtypeStruct((count, depth), jnp.bfloat16)]
        + [jax.ShapeDtypeStruct((2, count, piece), jnp.bfloat16)] * parts
        + [jax.ShapeDtypeStruct((2, depth, width), jnp.bfloat16)] * 2,
        (place, *blocks, gate_weight, up_weight),
        FLOPS,
        scratch=[pltpu.SemaphoreType.DMA((2,))] * 2,
    )
    return after, rows, result[:parts], result[parts], result[parts + 1]


def second(place, rows, blocks, part, up_now, after):
    half, depth = rows.shape
    size = blocks[0].shape[0]
    piece = part[0].shape[-1]
    count = half + size * len(blocks)

    def kernel(place_ref, after_ref, near_ref, up_ref, *refs):
        near_parts, refs = refs[: len(part)], refs[len(part) :]
        block_refs, (token_ref, rows_ref, *part_refs) = refs[: len(blocks)], refs[len(blocks) :]
        token_ref[...] = jnp.zeros_like(token_ref)
        for index, block_ref in enumerate(block_refs):
            rows_ref[half + index * size : half + (index + 1) * size, :] = block_ref[...]
        far_ref = rows_ref.at[half:count]
        project(far_ref, up_ref, [ref.at[:, half:count] for ref in part_refs], piece)
        rows_ref[0:half, :] = near_ref[...]
        for near_part, part_ref in zip(near_parts, part_refs):
            part_ref[:, 0:half, :] = near_part[...]

    after, rows, *result = call(
        kernel,
        "second",
        [held_whole()] * (3 + len(part) + len(blocks)),
        [TOKEN, jax.ShapeDtypeStruct((count, depth), jnp.bfloat16)]
        + [jax.ShapeDtypeStruct((2, count, piece), jnp.bfloat16)] * len(part),
        (place, after, rows, up_now, *part, *blocks),
    )
    return after, rows, result


def project(rows_ref, up_ref, part_refs, piece):
    for part, part_ref in enumerate(part_refs):
        for which in range(2):
            part_ref[which] = jnp.dot(
                rows_ref[...],
                up_ref[which, :, part * piece : (part + 1) * piece],
                preferred_element_type=jnp.float32,
            ).astype(jnp.bfloat16)


def work(place, after, step, width, parts, last, gate_weight, up_weight, down_weight, ups, downs, load_ups, load_downs):
    chunks = down_weight.shape[0] // width
    depth, outs = gate_weight.shape[0], down_weight.shape[1]
    piece = width // parts
    operands, specs = [place, after], [held_whole()]
    shapes, scratch, aliases = [TOKEN], [], {}
    if ups:
        operands += ups
        specs += [held_whole()] * 2
        shapes += [jax.ShapeDtypeStruct((2, ups[0].shape[0], piece), jnp.bfloat16)] * parts
    held_chunk, down, totals = downs if downs else ([], None, [])
    if downs:
        operands += [*held_chunk, down, *totals]
        specs += [held_whole()] * (len(held_chunk) + 1 + len(totals))
        for index, total in enumerate(totals):
            aliases[len(operands) - len(totals) + index] = len(shapes)
            shapes += [jax.ShapeDtypeStruct(total.shape, jnp.float32)]
    loads = []
    if load_ups:
        loads += [gate_weight, up_weight]
        shapes += [jax.ShapeDtypeStruct((2, depth, width), jnp.bfloat16)]
    if load_downs:
        loads += [down_weight]
        shapes += [jax.ShapeDtypeStruct((width, outs), jnp.bfloat16)]
    operands += loads
    specs += [pl.BlockSpec(memory_space=pltpu.HBM)] * len(loads)
    if loads:
        scratch = [pltpu.SemaphoreType.DMA((len(loads),))]

    def kernel(place_ref, after_ref, *refs):
        refs = list(refs)
        take = lambda number: [refs.pop(0) for _ in range(number)]
        rows_ref, up_ref = take(2) if ups else [None] * 2
        chunk_refs = take(len(held_chunk))
        (down_ref,) = take(1) if downs else [None]
        total_refs = take(len(totals))
        load_refs = take(len(loads))
        (token_ref,) = take(1)
        part_refs = take(parts) if ups else []
        out_refs = take(len(totals))
        (next_up,) = take(1) if load_ups else [None]
        (next_down,) = take(1) if load_downs else [None]
        added = jnp.clip(step + 2 - place_ref[0], 0, chunks - 1)
        held = step - 2 * last + place_ref[0]
        kept = jnp.clip(held + 1, 0, chunks - 1)
        pairs = []
        if load_ups:
            columns = pl.ds(pl.multiple_of(added * width, width), width)
            pairs += [(ref.at[:, columns], next_up.at[which]) for which, ref in enumerate(load_refs[:2])]
        if load_downs:
            pairs += [(load_refs[-1].at[pl.ds(pl.multiple_of(kept * width, width), width)], next_down)]
        copies = [pltpu.make_async_copy(*pair, refs[0].at[index]) for index, pair in enumerate(pairs)]
        for copy in copies:
            copy.start()
        token_ref[...] = jnp.zeros_like(token_ref)
        if ups:
            project(rows_ref, up_ref, part_refs, piece)
        if downs:

            @pl.when(jnp.logical_and(held >= 0, held < chunks))
            def _():
                terms = [jnp.dot(ref[...], down_ref[...], preferred_element_type=jnp.float32) for ref in chunk_refs]
                if len(terms) < len(totals):
                    terms = jnp.split(terms[0], len(totals))
                for out_ref, total_ref, term in zip(out_refs, total_refs, terms):
                    out_ref[...] = total_ref[...] + term

        for copy in copies:
            copy.wait()

    result = list(call(kernel, "work", specs, shapes, operands, FLOPS, aliases, scratch))
    after = result.pop(0)
    pieces = [result.pop(0) for _ in range(parts)] if ups else None
    totals = [result.pop(0) for _ in totals]
    next_up = result.pop(0) if load_ups else None
    return after, pieces, totals, next_up, result.pop(0) if load_downs else None


def combine(place, part, received, scales, after, step, index, last, sends, acts):
    _, count, piece = part.shape
    chunks = scales.shape[0]
    shapes = [TOKEN]
    if sends:
        shapes += [jax.ShapeDtypeStruct(part.shape, jnp.bfloat16)]
    if acts:
        shapes += [jax.ShapeDtypeStruct((count, piece), jnp.bfloat16)]

    def kernel(place_ref, part_ref, recv_ref, scale_ref, after_ref, token_ref, *refs):
        token_ref[...] = jnp.zeros_like(token_ref)
        sum_ref, hidden_ref = refs[0], refs[-1]

        if sends:

            @pl.when(place_ref[0] != last)
            def _():
                total = part_ref[...].astype(jnp.float32) + recv_ref[...].astype(jnp.float32)
                sum_ref[...] = total.astype(jnp.bfloat16)

        if acts:

            @pl.when(place_ref[0] == last)
            def _():
                chunk = min(max(step - last, 0), chunks - 1)
                columns = slice(index * piece, (index + 1) * piece)
                gate = part_ref[0].astype(jnp.float32) + recv_ref[0].astype(jnp.float32)
                up = part_ref[1].astype(jnp.float32) + recv_ref[1].astype(jnp.float32)
                g = gate * scale_ref[chunk, 0:1, columns]
                u = up * scale_ref[chunk, 1:2, columns]
                hidden_ref[...] = (jax.nn.silu(g) * u).astype(jnp.bfloat16)

    after, *result = call(
        kernel, "combine", [held_whole()] * 4, shapes, (place, part, received, scales, after)
    )
    return after, result[0] if sends else None, result[-1] if acts else None


def choose(place, pieces, received, after, last, cuts):
    count, width = received.shape
    piece = width // len(pieces)
    size = count // cuts

    def kernel(place_ref, recv_ref, after_ref, *refs):
        token_ref, *pass_refs = refs[len(pieces) :]
        token_ref[...] = jnp.zeros_like(token_ref)

        @pl.when(place_ref[0] == last)
        def _():
            for cut, pass_ref in enumerate(pass_refs):
                for index, piece_ref in enumerate(refs[: len(pieces)]):
                    pass_ref[:, index * piece : (index + 1) * piece] = piece_ref[cut * size : (cut + 1) * size, :]

        @pl.when(place_ref[0] != last)
        def _():
            for cut, pass_ref in enumerate(pass_refs):
                pass_ref[...] = recv_ref[cut * size : (cut + 1) * size, :]

    after, *chunk = call(
        kernel,
        "choose",
        [held_whole()] * (2 + len(pieces)),
        [TOKEN] + [jax.ShapeDtypeStruct((size, width), jnp.bfloat16)] * cuts,
        (place, received, after, *pieces),
    )
    return after, chunk


def swap(array, bit, size):
    return lax.ppermute(array, "gy", [(g, g ^ bit) for g in range(size)])


def gather(own, blocks, size):
    result = [own]
    for i in range(1, blocks):
        result.append(swap(result[i & (i - 1)], i & -i, size))
    return result


def scatter(total, blocks, size):
    bit = 1
    while bit < blocks:
        pairs = total.reshape(blocks // bit // 2, 2, -1, total.shape[-1])
        got = swap(pairs[:, 1].astype(jnp.bfloat16), bit, size)
        total = pairs[:, 0] + got.astype(jnp.float32)
        bit *= 2
    return total.reshape(-1, total.shape[-1])


def per_device(mesh, tokens, gate_weight, up_weight, gate_scale, up_scale, down_weight, down_scale):
    n_gx, n_gy = mesh.shape["gx"], mesh.shape["gy"]
    last = n_gx - 1
    units = gate_weight.shape[1]
    width = width_of(units)
    chunks = units // width
    order = {(q, g): (last - q if g % 2 == 0 else q) * n_gy + g for q in range(n_gx) for g in range(n_gy)}

    def onward(array, step):
        pairs = [(order[q, g], order[q + 1, g]) for q, g in order if q < last and 0 <= step - q < chunks]
        return lax.ppermute(array, ("gx", "gy"), pairs)

    def back(array, step):
        first = step - 2 * last
        pairs = [(order[q, g], order[q - 1, g]) for q, g in order if q > 0 and 0 <= first + q < chunks]
        return lax.ppermute(array, ("gx", "gy"), pairs)

    z, g = lax.axis_index("gx"), lax.axis_index("gy")
    place = jnp.where(g % 2 == 0, last - z, z).astype(jnp.int32).reshape(1)

    scales = jnp.stack([gate_scale.reshape(chunks, width), up_scale.reshape(chunks, width)], axis=1)

    summing, ending = chunks + last, chunks + 2 * last
    parts = 2 if width % 256 == 0 else 1

    def run(after, step, ups, downs, loads=True):
        return work(
            place, after, step, width, parts, last, gate_weight, up_weight, down_weight, ups, downs,
            loads and step + 2 < summing, loads and last <= step + 1 < ending,
        )

    steps, own, depth = tokens.shape
    mine = tokens.reshape(steps * own, depth)
    far = gather(swap(mine, n_gy // 2, n_gy), n_gy // 2, n_gy)
    near = gather(mine, n_gy // 2, n_gy)
    after, rows, part, up_now, up_next = first(place, near, gate_weight, up_weight, width, parts)
    after, rows, part = second(place, rows, far, part, up_now, after)
    count, outs = rows.shape[0], down_weight.shape[1]

    totals = [jnp.zeros((count // 2, outs), jnp.float32)] * 2
    got = [None] * parts
    held = [jnp.zeros((count, width), jnp.bfloat16)]
    down_next = None
    for step in range(ending):
        pieces = [None] * parts
        ups = None
        if step < summing:
            for index in range(parts):
                send = part[index]
                if step > 0:
                    after, send, pieces[index] = combine(
                        place, part[index], got[index], scales, after, step, index, last,
                        step + 1 < summing, step >= last,
                    )
                if step + 1 < summing:
                    got[index] = onward(send, step)
                    ups = [rows, up_next]
        if step < last:
            after, part, _, up_next, down_next = run(after, step, ups, None)
            continue
        chunk = held
        if step < summing:
            after, chunk = choose(place, pieces, held[0], after, last, 1 if step + 1 < summing else 2)
        if step + 1 < ending:
            held = [None] * len(chunk)
            for half in reversed(range(len(chunk))):
                held[half] = back(chunk[half], step)
        if step < summing:
            after, part, totals, up_next, down_next = run(after, step, ups, [chunk, down_next, totals])
        else:
            after, _, far, _, _ = run(after, step, None, [chunk[1:], down_next, totals[1:]], False)
            after, _, near, _, down_next = run(after, step, None, [chunk[:1], down_next, totals[:1]])
            totals = near + far

    far = scatter(totals[1], n_gy // 2, n_gy)
    got = swap(far.astype(jnp.bfloat16), n_gy // 2, n_gy)
    near = scatter(totals[0], n_gy // 2, n_gy)
    mixed = (near + got.astype(jnp.float32)).reshape(steps, own, outs) * down_scale
    return mixed.astype(jnp.bfloat16)


def solution(mesh):
    placed = (
        P(None, ("groups", "gy"), "gx"),
        P("gx", "gy"),
        P("gx", "gy"),
        P("gy"),
        P("gy"),
        P("gy", "gx"),
        P("gx"),
    )
    return jax.shard_map(
        functools.partial(per_device, mesh),
        mesh=mesh,
        in_specs=placed,
        out_specs=P(None, ("groups", "gy"), "gx"),
        check_vma=False,
    )
```

```python
import functools

import jax
import jax.numpy as jnp
from jax import lax
from jax.experimental import pallas as pl
from jax.experimental.pallas import tpu as pltpu
from jax.sharding import PartitionSpec as P

LIMIT = 28 * 1024 * 1024
FLOPS = 5_000_000_000
TOKEN = jax.ShapeDtypeStruct((8, 128), jnp.float32)


def width_of(units):
    return max(w for w in range(128, 513, 128) if units % w == 0)


def tile_of(size, limit):
    return max(t for t in range(128, min(size, limit) + 1, 128) if size % t == 0)


def held_whole():
    return pl.BlockSpec(memory_space=pltpu.VMEM)


def call(kernel, name, in_specs, out_shape, operands, flops=1, aliases={}, scratch=()):
    return pl.pallas_call(
        kernel,
        in_specs=[pl.BlockSpec(memory_space=pltpu.SMEM)] + in_specs,
        out_specs=[held_whole()] * len(out_shape),
        scratch_shapes=scratch,
        out_shape=out_shape,
        input_output_aliases=aliases,
        compiler_params=pltpu.CompilerParams(vmem_limit_bytes=LIMIT),
        cost_estimate=pl.CostEstimate(flops=flops, bytes_accessed=1, transcendentals=0),
        name=name,
    )(*operands)


def first(place, blocks, gate_weight, up_weight, width):
    size, depth = blocks[0].shape
    count = size * len(blocks)
    chunks = gate_weight.shape[1] // width

    def kernel(place_ref, *refs):
        block_refs, refs = refs[: len(blocks)], refs[len(blocks) :]
        weight_refs, (token_ref, rows_ref, part_ref, up_now, up_next, sem, next_sem) = refs[:2], refs[2:]
        added = jnp.clip(1 - place_ref[0], 0, chunks - 1)
        columns = pl.ds(pl.multiple_of(added * width, width), width)
        own, following = [], []
        for which, ref in enumerate(weight_refs):
            own.append(pltpu.make_async_copy(ref.at[:, 0:width], up_now.at[which], sem.at[which]))
            following.append(pltpu.make_async_copy(ref.at[:, columns], up_next.at[which], next_sem.at[which]))
        for copy in own + following:
            copy.start()
        token_ref[...] = jnp.zeros_like(token_ref)
        for index, block_ref in enumerate(block_refs):
            rows_ref[index * size : (index + 1) * size, :] = block_ref[...]
        for copy in own:
            copy.wait()
        project(rows_ref, up_now, [part_ref])
        for copy in following:
            copy.wait()

    return call(
        kernel,
        "first",
        [held_whole()] * len(blocks) + [pl.BlockSpec(memory_space=pltpu.HBM)] * 2,
        [TOKEN, jax.ShapeDtypeStruct((count, depth), jnp.bfloat16), jax.ShapeDtypeStruct((2, count, width), jnp.bfloat16)]
        + [jax.ShapeDtypeStruct((2, depth, width), jnp.bfloat16)] * 2,
        (place, *blocks, gate_weight, up_weight),
        FLOPS,
        scratch=[pltpu.SemaphoreType.DMA((2,))] * 2,
    )


def second(place, rows, blocks, up_now, after):
    half, depth = rows.shape
    size = blocks[0].shape[0]
    count = half + size * len(blocks)

    def kernel(place_ref, after_ref, near_ref, up_ref, *refs):
        block_refs, (token_ref, rows_ref, part_ref) = refs[: len(blocks)], refs[len(blocks) :]
        token_ref[...] = jnp.zeros_like(token_ref)
        for index, block_ref in enumerate(block_refs):
            rows_ref[half + index * size : half + (index + 1) * size, :] = block_ref[...]
        project(rows_ref.at[half:count], up_ref, [part_ref])
        rows_ref[0:half, :] = near_ref[...]

    return call(
        kernel,
        "second",
        [held_whole()] * (3 + len(blocks)),
        [
            TOKEN,
            jax.ShapeDtypeStruct((count, depth), jnp.bfloat16),
            jax.ShapeDtypeStruct((2, count - half, up_now.shape[-1]), jnp.bfloat16),
        ],
        (place, after, rows, up_now, *blocks),
    )


def project(rows_ref, up_ref, part_refs):
    for which in range(2):
        term = jnp.dot(rows_ref[...], up_ref[which], preferred_element_type=jnp.float32).astype(jnp.bfloat16)
        for part_ref, piece in zip(part_refs, jnp.split(term, len(part_refs))):
            part_ref[which] = piece


def work(place, after, step, width, parts, last, gate_weight, up_weight, down_weight, ups, downs, load_ups, load_downs):
    chunks = down_weight.shape[0] // width
    depth, outs = gate_weight.shape[0], down_weight.shape[1]
    operands, specs = [place, after], [held_whole()]
    shapes, scratch, aliases = [TOKEN], [], {}
    if ups:
        operands += ups
        specs += [held_whole()] * 2
        shapes += [jax.ShapeDtypeStruct((2, ups[0].shape[0] // parts, width), jnp.bfloat16)] * parts
    held_chunk, down, totals = downs if downs else ([], None, [])
    if downs:
        operands += [*held_chunk, down, *totals]
        specs += [held_whole()] * (len(held_chunk) + 1 + len(totals))
        for index, total in enumerate(totals):
            aliases[len(operands) - len(totals) + index] = len(shapes)
            shapes += [jax.ShapeDtypeStruct(total.shape, jnp.float32)]
    loads = []
    if load_ups:
        loads += [gate_weight, up_weight]
        shapes += [jax.ShapeDtypeStruct((2, depth, width), jnp.bfloat16)]
    if load_downs:
        loads += [down_weight]
        shapes += [jax.ShapeDtypeStruct((width, outs), jnp.bfloat16)]
    operands += loads
    specs += [pl.BlockSpec(memory_space=pltpu.HBM)] * len(loads)
    if loads:
        scratch = [pltpu.SemaphoreType.DMA((len(loads),))]

    def kernel(place_ref, after_ref, *refs):
        refs = list(refs)
        take = lambda number: [refs.pop(0) for _ in range(number)]
        rows_ref, up_ref = take(2) if ups else [None] * 2
        chunk_refs = take(len(held_chunk))
        (down_ref,) = take(1) if downs else [None]
        total_refs = take(len(totals))
        load_refs = take(len(loads))
        (token_ref,) = take(1)
        part_refs = take(parts) if ups else []
        out_refs = take(len(totals))
        (next_up,) = take(1) if load_ups else [None]
        (next_down,) = take(1) if load_downs else [None]
        added = jnp.clip(step + 2 - place_ref[0], 0, chunks - 1)
        held = step - 2 * last + place_ref[0]
        kept = jnp.clip(held + 1, 0, chunks - 1)
        pairs = []
        if load_ups:
            columns = pl.ds(pl.multiple_of(added * width, width), width)
            pairs += [(ref.at[:, columns], next_up.at[which]) for which, ref in enumerate(load_refs[:2])]
        if load_downs:
            pairs += [(load_refs[-1].at[pl.ds(pl.multiple_of(kept * width, width), width)], next_down)]
        copies = [pltpu.make_async_copy(*pair, refs[0].at[index]) for index, pair in enumerate(pairs)]
        for copy in copies:
            copy.start()
        token_ref[...] = jnp.zeros_like(token_ref)
        if ups:
            project(rows_ref, up_ref, part_refs)
        if downs:

            @pl.when(jnp.logical_and(held >= 0, held < chunks))
            def _():
                terms = [jnp.dot(ref[...], down_ref[...], preferred_element_type=jnp.float32) for ref in chunk_refs]
                if len(terms) < len(totals):
                    terms = jnp.split(terms[0], len(totals))
                for out_ref, total_ref, term in zip(out_refs, total_refs, terms):
                    out_ref[...] = total_ref[...] + term

        for copy in copies:
            copy.wait()

    result = list(call(kernel, "work", specs, shapes, operands, FLOPS, aliases, scratch))
    after = result.pop(0)
    pieces = [result.pop(0) for _ in range(parts)] if ups else None
    totals = [result.pop(0) for _ in totals]
    next_up = result.pop(0) if load_ups else None
    return after, pieces, totals, next_up, result.pop(0) if load_downs else None


def combine(place, part, received, scales, after, step, last, sends, acts):
    _, count, width = part.shape
    chunks = scales.shape[0]
    shapes = [TOKEN]
    if sends:
        shapes += [jax.ShapeDtypeStruct(part.shape, jnp.bfloat16)]
    if acts:
        shapes += [jax.ShapeDtypeStruct((count, width), jnp.bfloat16)]

    def kernel(place_ref, part_ref, recv_ref, scale_ref, after_ref, token_ref, *refs):
        token_ref[...] = jnp.zeros_like(token_ref)
        sum_ref, hidden_ref = refs[0], refs[-1]

        if sends:

            @pl.when(place_ref[0] != last)
            def _():
                total = part_ref[...].astype(jnp.float32) + recv_ref[...].astype(jnp.float32)
                sum_ref[...] = total.astype(jnp.bfloat16)

        if acts:

            @pl.when(place_ref[0] == last)
            def _():
                chunk = min(max(step - last, 0), chunks - 1)
                gate = part_ref[0].astype(jnp.float32) + recv_ref[0].astype(jnp.float32)
                up = part_ref[1].astype(jnp.float32) + recv_ref[1].astype(jnp.float32)
                g = gate * scale_ref[chunk, 0:1, :]
                u = up * scale_ref[chunk, 1:2, :]
                hidden_ref[...] = (jax.nn.silu(g) * u).astype(jnp.bfloat16)

    after, *result = call(
        kernel, "combine", [held_whole()] * 4, shapes, (place, part, received, scales, after)
    )
    return after, result[0] if sends else None, result[-1] if acts else None


def choose(place, pieces, received, after, last, cuts):
    count, width = received.shape
    size, own = count // cuts, count // len(pieces)

    def kernel(place_ref, recv_ref, after_ref, *refs):
        token_ref, *pass_refs = refs[len(pieces) :]
        token_ref[...] = jnp.zeros_like(token_ref)

        @pl.when(place_ref[0] == last)
        def _():
            for index, piece_ref in enumerate(refs[: len(pieces)]):
                cut, start = divmod(index * own, size)
                pass_refs[cut][start : start + own, :] = piece_ref[...]

        @pl.when(place_ref[0] != last)
        def _():
            for cut, pass_ref in enumerate(pass_refs):
                pass_ref[...] = recv_ref[cut * size : (cut + 1) * size, :]

    after, *chunk = call(
        kernel,
        "choose",
        [held_whole()] * (2 + len(pieces)),
        [TOKEN] + [jax.ShapeDtypeStruct((size, width), jnp.bfloat16)] * cuts,
        (place, received, after, *pieces),
    )
    return after, chunk


def swap(array, bit, size):
    return lax.ppermute(array, "gy", [(g, g ^ bit) for g in range(size)])


def gather(own, blocks, size):
    result = [own]
    for i in range(1, blocks):
        result.append(swap(result[i & (i - 1)], i & -i, size))
    return result


def hand_over(place, array, after):
    def kernel(place_ref, array_ref, after_ref, out_ref, token_ref):
        token_ref[...] = jnp.zeros_like(token_ref)
        out_ref[...] = array_ref[...]

    shapes = [jax.ShapeDtypeStruct(array.shape, array.dtype), TOKEN]
    return call(kernel, "hand_over", [held_whole()] * 2, shapes, (place, array, after))


def scatter(total, blocks, size):
    bit = 1
    while bit < blocks:
        pairs = total.reshape(blocks // bit // 2, 2, -1, total.shape[-1])
        got = swap(pairs[:, 1].astype(jnp.bfloat16), bit, size)
        total = pairs[:, 0] + got.astype(jnp.float32)
        bit *= 2
    return total.reshape(-1, total.shape[-1])


def per_device(mesh, tokens, gate_weight, up_weight, gate_scale, up_scale, down_weight, down_scale):
    n_gx, n_gy = mesh.shape["gx"], mesh.shape["gy"]
    last = n_gx - 1
    units = gate_weight.shape[1]
    width = width_of(units)
    chunks = units // width
    order = {(q, g): (last - q if g % 2 == 0 else q) * n_gy + g for q in range(n_gx) for g in range(n_gy)}

    def onward(array, step):
        pairs = [(order[q, g], order[q + 1, g]) for q, g in order if q < last and 0 <= step - q < chunks]
        return lax.ppermute(array, ("gx", "gy"), pairs)

    def back(array, step):
        first = step - 2 * last
        pairs = [(order[q, g], order[q - 1, g]) for q, g in order if q > 0 and 0 <= first + q < chunks]
        return lax.ppermute(array, ("gx", "gy"), pairs)

    z, g = lax.axis_index("gx"), lax.axis_index("gy")
    place = jnp.where(g % 2 == 0, last - z, z).astype(jnp.int32).reshape(1)

    scales = jnp.stack([gate_scale.reshape(chunks, width), up_scale.reshape(chunks, width)], axis=1)

    summing, ending = chunks + last, chunks + 2 * last
    parts = 2

    def run(after, step, ups, downs, loads=True):
        return work(
            place, after, step, width, parts, last, gate_weight, up_weight, down_weight, ups, downs,
            loads and step + 2 < summing, loads and last <= step + 1 < ending,
        )

    steps, own, depth = tokens.shape
    mine = tokens.reshape(steps * own, depth)
    further = swap(mine, n_gy // 2, n_gy)
    near = gather(mine, n_gy // 2, n_gy)
    after, rows, near_part, up_now, up_next = first(place, near, gate_weight, up_weight, width)
    further, after = hand_over(place, further, after)
    far = gather(further, n_gy // 2, n_gy)
    after, rows, far_part = second(place, rows, far, up_now, after)
    part = [near_part, far_part]
    count, outs = rows.shape[0], down_weight.shape[1]

    totals = [jnp.zeros((count // 2, outs), jnp.float32)] * 2
    got = [None] * parts
    held = [jnp.zeros((count, width), jnp.bfloat16)]
    down_next = None
    for step in range(ending):
        pieces = [None] * parts
        ups = None
        if step < summing:
            for index in range(parts):
                send = part[index]
                if step > 0:
                    after, send, pieces[index] = combine(
                        place, part[index], got[index], scales, after, step, last,
                        step + 1 < summing, step >= last,
                    )
                if step + 1 < summing:
                    got[index] = onward(send, step)
                    ups = [rows, up_next]
        if step < last:
            after, part, _, up_next, down_next = run(after, step, ups, None)
            continue
        chunk = held
        if step < summing:
            after, chunk = choose(place, pieces, held[0], after, last, 1 if step + 1 < summing else 2)
        if step + 1 < ending:
            held = [None] * len(chunk)
            for half in reversed(range(len(chunk))):
                held[half] = back(chunk[half], step)
        if step < summing:
            after, part, totals, up_next, down_next = run(after, step, ups, [chunk, down_next, totals])
        else:
            after, _, far, _, _ = run(after, step, None, [chunk[1:], down_next, totals[1:]], False)
            after, _, near, _, down_next = run(after, step, None, [chunk[:1], down_next, totals[:1]])
            totals = near + far

    far = scatter(totals[1], n_gy // 2, n_gy)
    got = swap(far.astype(jnp.bfloat16), n_gy // 2, n_gy)
    near = scatter(totals[0], n_gy // 2, n_gy)
    mixed = (near + got.astype(jnp.float32)).reshape(steps, own, outs) * down_scale
    return mixed.astype(jnp.bfloat16)


def solution(mesh):
    placed = (
        P(None, ("groups", "gy"), "gx"),
        P("gx", "gy"),
        P("gx", "gy"),
        P("gy"),
        P("gy"),
        P("gy", "gx"),
        P("gx"),
    )
    return jax.shard_map(
        functools.partial(per_device, mesh),
        mesh=mesh,
        in_specs=placed,
        out_specs=P(None, ("groups", "gy"), "gx"),
        check_vma=False,
    )
```

```python
import functools

import jax
import jax.numpy as jnp
from jax import lax
from jax.experimental import pallas as pl
from jax.experimental.pallas import tpu as pltpu
from jax.sharding import PartitionSpec as P

LIMIT = 28 * 1024 * 1024
FLOPS = 5_000_000_000
TOKEN = jax.ShapeDtypeStruct((8, 128), jnp.float32)


def width_of(units):
    return max(w for w in range(128, 513, 128) if units % w == 0)


def tile_of(size, limit):
    return max(t for t in range(128, min(size, limit) + 1, 128) if size % t == 0)


def held_whole():
    return pl.BlockSpec(memory_space=pltpu.VMEM)


def call(kernel, name, in_specs, out_shape, operands, flops=1, aliases={}, scratch=()):
    return pl.pallas_call(
        kernel,
        in_specs=[pl.BlockSpec(memory_space=pltpu.SMEM)] + in_specs,
        out_specs=[held_whole()] * len(out_shape),
        scratch_shapes=scratch,
        out_shape=out_shape,
        input_output_aliases=aliases,
        compiler_params=pltpu.CompilerParams(vmem_limit_bytes=LIMIT),
        cost_estimate=pl.CostEstimate(flops=flops, bytes_accessed=1, transcendentals=0),
        name=name,
    )(*operands)


def first(place, blocks, gate_weight, up_weight, width):
    size, depth = blocks[0].shape
    count = size * len(blocks)
    chunks = gate_weight.shape[1] // width

    def kernel(place_ref, *refs):
        block_refs, refs = refs[: len(blocks)], refs[len(blocks) :]
        weight_refs, (token_ref, rows_ref, part_ref, up_now, up_next, sem, next_sem) = refs[:2], refs[2:]
        added = jnp.clip(1 - place_ref[0], 0, chunks - 1)
        columns = pl.ds(pl.multiple_of(added * width, width), width)
        own, following = [], []
        for which, ref in enumerate(weight_refs):
            own.append(pltpu.make_async_copy(ref.at[:, 0:width], up_now.at[which], sem.at[which]))
            following.append(pltpu.make_async_copy(ref.at[:, columns], up_next.at[which], next_sem.at[which]))
        for copy in own + following:
            copy.start()
        token_ref[...] = jnp.zeros_like(token_ref)
        for index, block_ref in enumerate(block_refs):
            rows_ref[index * size : (index + 1) * size, :] = block_ref[...]
        for copy in own:
            copy.wait()
        project(rows_ref, up_now, [part_ref])
        for copy in following:
            copy.wait()

    return call(
        kernel,
        "first",
        [held_whole()] * len(blocks) + [pl.BlockSpec(memory_space=pltpu.HBM)] * 2,
        [TOKEN, jax.ShapeDtypeStruct((count, depth), jnp.bfloat16), jax.ShapeDtypeStruct((2, count, width), jnp.bfloat16)]
        + [jax.ShapeDtypeStruct((2, depth, width), jnp.bfloat16)] * 2,
        (place, *blocks, gate_weight, up_weight),
        FLOPS,
        scratch=[pltpu.SemaphoreType.DMA((2,))] * 2,
    )


def second(place, rows, blocks, up_now, after):
    half, depth = rows.shape
    size = blocks[0].shape[0]
    count = half + size * len(blocks)

    def kernel(place_ref, after_ref, near_ref, up_ref, *refs):
        block_refs, (token_ref, rows_ref, part_ref) = refs[: len(blocks)], refs[len(blocks) :]
        token_ref[...] = jnp.zeros_like(token_ref)
        for index, block_ref in enumerate(block_refs):
            rows_ref[half + index * size : half + (index + 1) * size, :] = block_ref[...]
        project(rows_ref.at[half:count], up_ref, [part_ref])
        rows_ref[0:half, :] = near_ref[...]

    return call(
        kernel,
        "second",
        [held_whole()] * (3 + len(blocks)),
        [
            TOKEN,
            jax.ShapeDtypeStruct((count, depth), jnp.bfloat16),
            jax.ShapeDtypeStruct((2, count - half, up_now.shape[-1]), jnp.bfloat16),
        ],
        (place, after, rows, up_now, *blocks),
    )


def project(rows_ref, up_ref, part_refs):
    for which in range(2):
        term = jnp.dot(rows_ref[...], up_ref[which], preferred_element_type=jnp.float32).astype(jnp.bfloat16)
        for part_ref, piece in zip(part_refs, jnp.split(term, len(part_refs))):
            part_ref[which] = piece


def work(place, after, step, width, parts, last, gate_weight, up_weight, down_weight, ups, downs, load_ups, load_downs):
    chunks = down_weight.shape[0] // width
    depth, outs = gate_weight.shape[0], down_weight.shape[1]
    operands, specs = [place, after], [held_whole()]
    shapes, scratch, aliases = [TOKEN], [], {}
    if ups:
        operands += ups
        specs += [held_whole()] * 2
        shapes += [jax.ShapeDtypeStruct((2, ups[0].shape[0] // parts, width), jnp.bfloat16)] * parts
    held_chunk, down, totals = downs if downs else ([], None, [])
    if downs:
        operands += [*held_chunk, down, *totals]
        specs += [held_whole()] * (len(held_chunk) + 1 + len(totals))
        for index, total in enumerate(totals):
            aliases[len(operands) - len(totals) + index] = len(shapes)
            shapes += [jax.ShapeDtypeStruct(total.shape, jnp.float32)]
    loads = []
    if load_ups:
        loads += [gate_weight, up_weight]
        shapes += [jax.ShapeDtypeStruct((2, depth, width), jnp.bfloat16)]
    if load_downs:
        loads += [down_weight]
        shapes += [jax.ShapeDtypeStruct((width, outs), jnp.bfloat16)]
    operands += loads
    specs += [pl.BlockSpec(memory_space=pltpu.HBM)] * len(loads)
    if loads:
        scratch = [pltpu.SemaphoreType.DMA((len(loads),))]

    def kernel(place_ref, after_ref, *refs):
        refs = list(refs)
        take = lambda number: [refs.pop(0) for _ in range(number)]
        rows_ref, up_ref = take(2) if ups else [None] * 2
        chunk_refs = take(len(held_chunk))
        (down_ref,) = take(1) if downs else [None]
        total_refs = take(len(totals))
        load_refs = take(len(loads))
        (token_ref,) = take(1)
        part_refs = take(parts) if ups else []
        out_refs = take(len(totals))
        (next_up,) = take(1) if load_ups else [None]
        (next_down,) = take(1) if load_downs else [None]
        added = jnp.clip(step + 2 - place_ref[0], 0, chunks - 1)
        held = step - 2 * last + place_ref[0]
        kept = jnp.clip(held + 1, 0, chunks - 1)
        pairs = []
        if load_ups:
            columns = pl.ds(pl.multiple_of(added * width, width), width)
            pairs += [(ref.at[:, columns], next_up.at[which]) for which, ref in enumerate(load_refs[:2])]
        if load_downs:
            pairs += [(load_refs[-1].at[pl.ds(pl.multiple_of(kept * width, width), width)], next_down)]
        copies = [pltpu.make_async_copy(*pair, refs[0].at[index]) for index, pair in enumerate(pairs)]
        for copy in reversed(copies) if downs else copies:
            copy.start()
        token_ref[...] = jnp.zeros_like(token_ref)
        if downs:

            @pl.when(jnp.logical_and(held >= 0, held < chunks))
            def _():
                share = len(totals) // len(chunk_refs)
                for index, (out_ref, total_ref) in enumerate(zip(out_refs, total_refs)):
                    size, start = total_ref.shape[0], index % share * total_ref.shape[0]
                    chunk = chunk_refs[index // share][start : start + size, :]
                    out_ref[...] = total_ref[...] + jnp.dot(chunk, down_ref[...], preferred_element_type=jnp.float32)

        if ups:
            project(rows_ref, up_ref, part_refs)
        for copy in copies:
            copy.wait()

    result = list(call(kernel, "work", specs, shapes, operands, FLOPS, aliases, scratch))
    after = result.pop(0)
    pieces = [result.pop(0) for _ in range(parts)] if ups else None
    totals = [result.pop(0) for _ in totals]
    next_up = result.pop(0) if load_ups else None
    return after, pieces, totals, next_up, result.pop(0) if load_downs else None


def combine(place, part, received, scales, after, step, last, sends, acts):
    _, count, width = part.shape
    chunks = scales.shape[0]
    shapes = [TOKEN]
    if sends:
        shapes += [jax.ShapeDtypeStruct(part.shape, jnp.bfloat16)]
    if acts:
        shapes += [jax.ShapeDtypeStruct((count, width), jnp.bfloat16)]

    def kernel(place_ref, part_ref, recv_ref, scale_ref, after_ref, token_ref, *refs):
        token_ref[...] = jnp.zeros_like(token_ref)
        sum_ref, hidden_ref = refs[0], refs[-1]

        if sends:

            @pl.when(place_ref[0] != last)
            def _():
                total = part_ref[...].astype(jnp.float32) + recv_ref[...].astype(jnp.float32)
                sum_ref[...] = total.astype(jnp.bfloat16)

        if acts:

            @pl.when(place_ref[0] == last)
            def _():
                chunk = min(max(step - last, 0), chunks - 1)
                gate = part_ref[0].astype(jnp.float32) + recv_ref[0].astype(jnp.float32)
                up = part_ref[1].astype(jnp.float32) + recv_ref[1].astype(jnp.float32)
                g = gate * scale_ref[chunk, 0:1, :]
                u = up * scale_ref[chunk, 1:2, :]
                hidden_ref[...] = (jax.nn.silu(g) * u).astype(jnp.bfloat16)

    after, *result = call(
        kernel, "combine", [held_whole()] * 4, shapes, (place, part, received, scales, after)
    )
    return after, result[0] if sends else None, result[-1] if acts else None


def choose(place, pieces, received, after, last, cuts):
    count, width = received.shape
    size, own = count // cuts, count // len(pieces)

    def kernel(place_ref, recv_ref, after_ref, *refs):
        token_ref, *pass_refs = refs[len(pieces) :]
        token_ref[...] = jnp.zeros_like(token_ref)

        @pl.when(place_ref[0] == last)
        def _():
            for index, piece_ref in enumerate(refs[: len(pieces)]):
                cut, start = divmod(index * own, size)
                pass_refs[cut][start : start + own, :] = piece_ref[...]

        @pl.when(place_ref[0] != last)
        def _():
            for cut, pass_ref in enumerate(pass_refs):
                pass_ref[...] = recv_ref[cut * size : (cut + 1) * size, :]

    after, *chunk = call(
        kernel,
        "choose",
        [held_whole()] * (2 + len(pieces)),
        [TOKEN] + [jax.ShapeDtypeStruct((size, width), jnp.bfloat16)] * cuts,
        (place, received, after, *pieces),
    )
    return after, chunk


def swap(array, bit, size):
    return lax.ppermute(array, "gy", [(g, g ^ bit) for g in range(size)])


def gather(own, blocks, size):
    result = [own]
    for i in range(1, blocks):
        result.append(swap(result[i & (i - 1)], i & -i, size))
    return result


def hand_over(place, array, after):
    def kernel(place_ref, array_ref, after_ref, out_ref, token_ref):
        token_ref[...] = jnp.zeros_like(token_ref)
        out_ref[...] = array_ref[...]

    shapes = [jax.ShapeDtypeStruct(array.shape, array.dtype), TOKEN]
    return call(kernel, "hand_over", [held_whole()] * 2, shapes, (place, array, after))


def scatter(total, blocks, size):
    bit = 1
    while bit < blocks:
        pairs = total.reshape(blocks // bit // 2, 2, -1, total.shape[-1])
        got = swap(pairs[:, 1].astype(jnp.bfloat16), bit, size)
        total = pairs[:, 0] + got.astype(jnp.float32)
        bit *= 2
    return total.reshape(-1, total.shape[-1])


def per_device(mesh, tokens, gate_weight, up_weight, gate_scale, up_scale, down_weight, down_scale):
    n_gx, n_gy = mesh.shape["gx"], mesh.shape["gy"]
    last = n_gx - 1
    units = gate_weight.shape[1]
    width = width_of(units)
    chunks = units // width
    order = {(q, g): (last - q if g % 2 == 0 else q) * n_gy + g for q in range(n_gx) for g in range(n_gy)}

    def onward(array, step):
        pairs = [(order[q, g], order[q + 1, g]) for q, g in order if q < last and 0 <= step - q < chunks]
        return lax.ppermute(array, ("gx", "gy"), pairs)

    def back(array, step):
        first = step - 2 * last
        pairs = [(order[q, g], order[q - 1, g]) for q, g in order if q > 0 and 0 <= first + q < chunks]
        return lax.ppermute(array, ("gx", "gy"), pairs)

    z, g = lax.axis_index("gx"), lax.axis_index("gy")
    place = jnp.where(g % 2 == 0, last - z, z).astype(jnp.int32).reshape(1)

    scales = jnp.stack([gate_scale.reshape(chunks, width), up_scale.reshape(chunks, width)], axis=1)

    summing, ending = chunks + last, chunks + 2 * last
    parts = 2

    def run(after, step, ups, downs, loads=True):
        return work(
            place, after, step, width, parts, last, gate_weight, up_weight, down_weight, ups, downs,
            loads and step + 2 < summing, loads and last <= step + 1 < ending,
        )

    steps, own, depth = tokens.shape
    mine = tokens.reshape(steps * own, depth)
    further = swap(mine, n_gy // 2, n_gy)
    near = gather(mine, n_gy // 2, n_gy)
    after, rows, near_part, up_now, up_next = first(place, near, gate_weight, up_weight, width)
    further, after = hand_over(place, further, after)
    far = gather(further, n_gy // 2, n_gy)
    after, rows, far_part = second(place, rows, far, up_now, after)
    part = [near_part, far_part]
    count, outs = rows.shape[0], down_weight.shape[1]

    totals = [jnp.zeros((count // 2, outs), jnp.float32)] * 2
    got = [None] * parts
    held = [jnp.zeros((count, width), jnp.bfloat16)]
    down_next = None
    for step in range(ending):
        pieces = [None] * parts
        ups = None
        if step < summing:
            for index in range(parts):
                send = part[index]
                if step > 0:
                    after, send, pieces[index] = combine(
                        place, part[index], got[index], scales, after, step, last,
                        step + 1 < summing, step >= last,
                    )
                if step + 1 < summing:
                    got[index] = onward(send, step)
                    ups = [rows, up_next]
        if step < last:
            after, part, _, up_next, down_next = run(after, step, ups, None)
            continue
        chunk = held
        if step < summing:
            after, chunk = choose(place, pieces, held[0], after, last, 1 if step + 1 < summing else 2)
        if step + 1 < ending:
            held = [None] * len(chunk)
            for half in reversed(range(len(chunk))):
                held[half] = back(chunk[half], step)
        if step < summing:
            after, part, totals, up_next, down_next = run(after, step, ups, [chunk, down_next, totals])
        else:
            after, _, far, _, _ = run(after, step, None, [chunk[1:], down_next, totals[1:]], False)
            after, _, near, _, down_next = run(after, step, None, [chunk[:1], down_next, totals[:1]])
            totals = near + far

    far = scatter(totals[1], n_gy // 2, n_gy)
    got = swap(far.astype(jnp.bfloat16), n_gy // 2, n_gy)
    near = scatter(totals[0], n_gy // 2, n_gy)
    mixed = (near + got.astype(jnp.float32)).reshape(steps, own, outs) * down_scale
    return mixed.astype(jnp.bfloat16)


def solution(mesh):
    placed = (
        P(None, ("groups", "gy"), "gx"),
        P("gx", "gy"),
        P("gx", "gy"),
        P("gy"),
        P("gy"),
        P("gy", "gx"),
        P("gx"),
    )
    return jax.shard_map(
        functools.partial(per_device, mesh),
        mesh=mesh,
        in_specs=placed,
        out_specs=P(None, ("groups", "gy"), "gx"),
        check_vma=False,
    )
```

```python
import functools

import jax
import jax.numpy as jnp
from jax import lax
from jax.experimental import pallas as pl
from jax.experimental.pallas import tpu as pltpu
from jax.sharding import PartitionSpec as P

LIMIT = 28 * 1024 * 1024
FLOPS = 5_000_000_000
TOKEN = jax.ShapeDtypeStruct((8, 128), jnp.float32)


def width_of(units):
    return max(w for w in range(128, 513, 128) if units % w == 0)


def tile_of(size, limit):
    return max(t for t in range(128, min(size, limit) + 1, 128) if size % t == 0)


def held_whole():
    return pl.BlockSpec(memory_space=pltpu.VMEM)


def call(kernel, name, in_specs, out_shape, operands, flops=1, aliases={}, scratch=()):
    return pl.pallas_call(
        kernel,
        in_specs=[pl.BlockSpec(memory_space=pltpu.SMEM)] + in_specs,
        out_specs=[held_whole()] * len(out_shape),
        scratch_shapes=scratch,
        out_shape=out_shape,
        input_output_aliases=aliases,
        compiler_params=pltpu.CompilerParams(vmem_limit_bytes=LIMIT),
        cost_estimate=pl.CostEstimate(flops=flops, bytes_accessed=1, transcendentals=0),
        name=name,
    )(*operands)


def first(place, blocks, gate_weight, up_weight, width):
    size, depth = blocks[0].shape
    count = size * len(blocks)
    chunks = gate_weight.shape[1] // width

    def kernel(place_ref, *refs):
        block_refs, refs = refs[: len(blocks)], refs[len(blocks) :]
        weight_refs, (token_ref, rows_ref, part_ref, up_next, up_now, sem, next_sem) = refs[:2], refs[2:]
        added = jnp.clip(1 - place_ref[0], 0, chunks - 1)
        columns = pl.ds(pl.multiple_of(added * width, width), width)
        own, following = [], []
        for which, ref in enumerate(weight_refs):
            own.append(pltpu.make_async_copy(ref.at[:, 0:width], up_now.at[which], sem.at[which]))
            following.append(pltpu.make_async_copy(ref.at[:, columns], up_next.at[which], next_sem.at[which]))
        for copy in own + following:
            copy.start()
        token_ref[...] = jnp.zeros_like(token_ref)
        for index, block_ref in enumerate(block_refs):
            rows_ref[index * size : (index + 1) * size, :] = block_ref[...]
        for copy in own:
            copy.wait()
        project(rows_ref, up_now, [part_ref])
        for copy in following:
            copy.wait()

    return call(
        kernel,
        "first",
        [held_whole()] * len(blocks) + [pl.BlockSpec(memory_space=pltpu.HBM)] * 2,
        [TOKEN, jax.ShapeDtypeStruct((count, depth), jnp.bfloat16), jax.ShapeDtypeStruct((2, count, width), jnp.bfloat16)]
        + [jax.ShapeDtypeStruct((2, depth, width), jnp.bfloat16)],
        (place, *blocks, gate_weight, up_weight),
        FLOPS,
        scratch=[pltpu.VMEM((2, depth, width), jnp.bfloat16)] + [pltpu.SemaphoreType.DMA((2,))] * 2,
    )


def load(place, gate_weight, up_weight, after, width):
    def kernel(place_ref, after_ref, gate_ref, up_ref, token_ref, up_now, sem):
        token_ref[...] = jnp.zeros_like(token_ref)
        copies = [
            pltpu.make_async_copy(ref.at[:, 0:width], up_now.at[which], sem.at[which])
            for which, ref in enumerate([gate_ref, up_ref])
        ]
        for copy in copies:
            copy.start()
        for copy in copies:
            copy.wait()

    return call(
        kernel,
        "load",
        [held_whole()] + [pl.BlockSpec(memory_space=pltpu.HBM)] * 2,
        [TOKEN, jax.ShapeDtypeStruct((2, gate_weight.shape[0], width), jnp.bfloat16)],
        (place, after, gate_weight, up_weight),
        FLOPS,
        scratch=[pltpu.SemaphoreType.DMA((2,))],
    )


def second(place, rows, blocks, up_now, after):
    half, depth = rows.shape
    size = blocks[0].shape[0]
    count = half + size * len(blocks)

    def kernel(place_ref, after_ref, near_ref, up_ref, *refs):
        block_refs, (token_ref, rows_ref, part_ref) = refs[: len(blocks)], refs[len(blocks) :]
        token_ref[...] = jnp.zeros_like(token_ref)
        for index, block_ref in enumerate(block_refs):
            rows_ref[half + index * size : half + (index + 1) * size, :] = block_ref[...]
        project(rows_ref.at[half:count], up_ref, [part_ref])
        rows_ref[0:half, :] = near_ref[...]

    return call(
        kernel,
        "second",
        [held_whole()] * (3 + len(blocks)),
        [
            TOKEN,
            jax.ShapeDtypeStruct((count, depth), jnp.bfloat16),
            jax.ShapeDtypeStruct((2, count - half, up_now.shape[-1]), jnp.bfloat16),
        ],
        (place, after, rows, up_now, *blocks),
    )


def project(rows_ref, up_ref, part_refs):
    for which in range(2):
        term = jnp.dot(rows_ref[...], up_ref[which], preferred_element_type=jnp.float32).astype(jnp.bfloat16)
        for part_ref, piece in zip(part_refs, jnp.split(term, len(part_refs))):
            part_ref[which] = piece


def work(place, after, step, width, parts, last, gate_weight, up_weight, down_weight, ups, downs, load_ups, load_downs):
    chunks = down_weight.shape[0] // width
    depth, outs = gate_weight.shape[0], down_weight.shape[1]
    operands, specs = [place, after], [held_whole()]
    shapes, scratch, aliases = [TOKEN], [], {}
    if ups:
        operands += ups
        specs += [held_whole()] * 2
        shapes += [jax.ShapeDtypeStruct((2, ups[0].shape[0] // parts, width), jnp.bfloat16)] * parts
    held_chunk, down, totals = downs if downs else ([], None, [])
    if downs:
        operands += [*held_chunk, down, *totals]
        specs += [held_whole()] * (len(held_chunk) + 1 + len(totals))
        for index, total in enumerate(totals):
            aliases[len(operands) - len(totals) + index] = len(shapes)
            shapes += [jax.ShapeDtypeStruct(total.shape, jnp.float32)]
    loads = []
    if load_ups:
        loads += [gate_weight, up_weight]
        shapes += [jax.ShapeDtypeStruct((2, depth, width), jnp.bfloat16)]
    if load_downs:
        loads += [down_weight]
        shapes += [jax.ShapeDtypeStruct((width, outs), jnp.bfloat16)]
    operands += loads
    specs += [pl.BlockSpec(memory_space=pltpu.HBM)] * len(loads)
    if loads:
        scratch = [pltpu.SemaphoreType.DMA((len(loads),))]

    def kernel(place_ref, after_ref, *refs):
        refs = list(refs)
        take = lambda number: [refs.pop(0) for _ in range(number)]
        rows_ref, up_ref = take(2) if ups else [None] * 2
        chunk_refs = take(len(held_chunk))
        (down_ref,) = take(1) if downs else [None]
        total_refs = take(len(totals))
        load_refs = take(len(loads))
        (token_ref,) = take(1)
        part_refs = take(parts) if ups else []
        out_refs = take(len(totals))
        (next_up,) = take(1) if load_ups else [None]
        (next_down,) = take(1) if load_downs else [None]
        added = jnp.clip(step + 2 - place_ref[0], 0, chunks - 1)
        held = step - 2 * last + place_ref[0]
        kept = jnp.clip(held + 1, 0, chunks - 1)
        pairs = []
        if load_ups:
            columns = pl.ds(pl.multiple_of(added * width, width), width)
            pairs += [(ref.at[:, columns], next_up.at[which]) for which, ref in enumerate(load_refs[:2])]
        if load_downs:
            pairs += [(load_refs[-1].at[pl.ds(pl.multiple_of(kept * width, width), width)], next_down)]
        copies = [pltpu.make_async_copy(*pair, refs[0].at[index]) for index, pair in enumerate(pairs)]
        for copy in reversed(copies) if downs else copies:
            copy.start()
        token_ref[...] = jnp.zeros_like(token_ref)
        if downs:

            @pl.when(jnp.logical_and(held >= 0, held < chunks))
            def _():
                share = len(totals) // len(chunk_refs)
                for index, (out_ref, total_ref) in enumerate(zip(out_refs, total_refs)):
                    size, start = total_ref.shape[0], index % share * total_ref.shape[0]
                    chunk = chunk_refs[index // share][start : start + size, :]
                    out_ref[...] = total_ref[...] + jnp.dot(chunk, down_ref[...], preferred_element_type=jnp.float32)

        if ups:
            project(rows_ref, up_ref, part_refs)
        for copy in copies:
            copy.wait()

    result = list(call(kernel, "work", specs, shapes, operands, FLOPS, aliases, scratch))
    after = result.pop(0)
    pieces = [result.pop(0) for _ in range(parts)] if ups else None
    totals = [result.pop(0) for _ in totals]
    next_up = result.pop(0) if load_ups else None
    return after, pieces, totals, next_up, result.pop(0) if load_downs else None


def combine(place, part, received, scales, after, step, last, sends, acts):
    _, count, width = part.shape
    chunks = scales.shape[0]
    shapes = [TOKEN]
    if sends:
        shapes += [jax.ShapeDtypeStruct(part.shape, jnp.bfloat16)]
    if acts:
        shapes += [jax.ShapeDtypeStruct((count, width), jnp.bfloat16)]

    def kernel(place_ref, part_ref, recv_ref, scale_ref, after_ref, token_ref, *refs):
        token_ref[...] = jnp.zeros_like(token_ref)
        sum_ref, hidden_ref = refs[0], refs[-1]

        if sends:

            @pl.when(place_ref[0] != last)
            def _():
                total = part_ref[...].astype(jnp.float32) + recv_ref[...].astype(jnp.float32)
                sum_ref[...] = total.astype(jnp.bfloat16)

        if acts:

            @pl.when(place_ref[0] == last)
            def _():
                chunk = min(max(step - last, 0), chunks - 1)
                gate = part_ref[0].astype(jnp.float32) + recv_ref[0].astype(jnp.float32)
                up = part_ref[1].astype(jnp.float32) + recv_ref[1].astype(jnp.float32)
                g = gate * scale_ref[chunk, 0:1, :]
                u = up * scale_ref[chunk, 1:2, :]
                hidden_ref[...] = (jax.nn.silu(g) * u).astype(jnp.bfloat16)

    after, *result = call(
        kernel, "combine", [held_whole()] * 4, shapes, (place, part, received, scales, after)
    )
    return after, result[0] if sends else None, result[-1] if acts else None


def choose(place, pieces, received, after, last, cuts):
    count, width = received.shape
    size, own = count // cuts, count // len(pieces)

    def kernel(place_ref, recv_ref, after_ref, *refs):
        token_ref, *pass_refs = refs[len(pieces) :]
        token_ref[...] = jnp.zeros_like(token_ref)

        @pl.when(place_ref[0] == last)
        def _():
            for index, piece_ref in enumerate(refs[: len(pieces)]):
                cut, start = divmod(index * own, size)
                pass_refs[cut][start : start + own, :] = piece_ref[...]

        @pl.when(place_ref[0] != last)
        def _():
            for cut, pass_ref in enumerate(pass_refs):
                pass_ref[...] = recv_ref[cut * size : (cut + 1) * size, :]

    after, *chunk = call(
        kernel,
        "choose",
        [held_whole()] * (2 + len(pieces)),
        [TOKEN] + [jax.ShapeDtypeStruct((size, width), jnp.bfloat16)] * cuts,
        (place, received, after, *pieces),
    )
    return after, chunk


def swap(array, bit, size):
    return lax.ppermute(array, "gy", [(g, g ^ bit) for g in range(size)])


def gather(own, blocks, size):
    result = [own]
    for i in range(1, blocks):
        result.append(swap(result[i & (i - 1)], i & -i, size))
    return result


def hand_over(place, array, after):
    def kernel(place_ref, array_ref, after_ref, out_ref, token_ref):
        token_ref[...] = jnp.zeros_like(token_ref)
        out_ref[...] = array_ref[...]

    shapes = [jax.ShapeDtypeStruct(array.shape, array.dtype), TOKEN]
    return call(kernel, "hand_over", [held_whole()] * 2, shapes, (place, array, after))


def scatter(total, blocks, size):
    bit = 1
    while bit < blocks:
        pairs = total.reshape(blocks // bit // 2, 2, -1, total.shape[-1])
        got = swap(pairs[:, 1].astype(jnp.bfloat16), bit, size)
        total = pairs[:, 0] + got.astype(jnp.float32)
        bit *= 2
    return total.reshape(-1, total.shape[-1])


def per_device(mesh, tokens, gate_weight, up_weight, gate_scale, up_scale, down_weight, down_scale):
    n_gx, n_gy = mesh.shape["gx"], mesh.shape["gy"]
    last = n_gx - 1
    units = gate_weight.shape[1]
    width = width_of(units)
    chunks = units // width
    order = {(q, g): (last - q if g % 2 == 0 else q) * n_gy + g for q in range(n_gx) for g in range(n_gy)}

    def onward(array, step):
        pairs = [(order[q, g], order[q + 1, g]) for q, g in order if q < last and 0 <= step - q < chunks]
        return lax.ppermute(array, ("gx", "gy"), pairs)

    def back(array, step):
        first = step - 2 * last
        pairs = [(order[q, g], order[q - 1, g]) for q, g in order if q > 0 and 0 <= first + q < chunks]
        return lax.ppermute(array, ("gx", "gy"), pairs)

    z, g = lax.axis_index("gx"), lax.axis_index("gy")
    place = jnp.where(g % 2 == 0, last - z, z).astype(jnp.int32).reshape(1)

    scales = jnp.stack([gate_scale.reshape(chunks, width), up_scale.reshape(chunks, width)], axis=1)

    summing, ending = chunks + last, chunks + 2 * last
    parts = 2

    def run(after, step, ups, downs, loads=True):
        return work(
            place, after, step, width, parts, last, gate_weight, up_weight, down_weight, ups, downs,
            loads and step + 2 < summing, loads and last <= step + 1 < ending,
        )

    steps, own, depth = tokens.shape
    mine = tokens.reshape(steps * own, depth)
    further = swap(mine, n_gy // 2, n_gy)
    near = gather(mine, n_gy // 2, n_gy)
    after, rows, near_part, up_next = first(place, near, gate_weight, up_weight, width)
    further, after = hand_over(place, further, after)
    far = gather(further, n_gy // 2, n_gy)
    after, up_now = load(place, gate_weight, up_weight, after, width)
    after, rows, far_part = second(place, rows, far, up_now, after)
    part = [near_part, far_part]
    count, outs = rows.shape[0], down_weight.shape[1]

    totals = [jnp.zeros((count // 2, outs), jnp.float32)] * 2
    got = [None] * parts
    held = [jnp.zeros((count, width), jnp.bfloat16)]
    down_next = None
    for step in range(ending):
        pieces = [None] * parts
        ups = None
        if step < summing:
            for index in range(parts):
                send = part[index]
                if step > 0:
                    after, send, pieces[index] = combine(
                        place, part[index], got[index], scales, after, step, last,
                        step + 1 < summing, step >= last,
                    )
                if step + 1 < summing:
                    got[index] = onward(send, step)
                    ups = [rows, up_next]
        if step < last:
            after, part, _, up_next, down_next = run(after, step, ups, None)
            continue
        chunk = held
        if step < summing:
            after, chunk = choose(place, pieces, held[0], after, last, 1 if step + 1 < summing else 2)
        if step + 1 < ending:
            held = [None] * len(chunk)
            for half in reversed(range(len(chunk))):
                held[half] = back(chunk[half], step)
        if step < summing:
            after, part, totals, up_next, down_next = run(after, step, ups, [chunk, down_next, totals])
        else:
            after, _, far, _, _ = run(after, step, None, [chunk[1:], down_next, totals[1:]], False)
            after, _, near, _, down_next = run(after, step, None, [chunk[:1], down_next, totals[:1]])
            totals = near + far

    far = scatter(totals[1], n_gy // 2, n_gy)
    got = swap(far.astype(jnp.bfloat16), n_gy // 2, n_gy)
    near = scatter(totals[0], n_gy // 2, n_gy)
    mixed = (near + got.astype(jnp.float32)).reshape(steps, own, outs) * down_scale
    return mixed.astype(jnp.bfloat16)


def solution(mesh):
    placed = (
        P(None, ("groups", "gy"), "gx"),
        P("gx", "gy"),
        P("gx", "gy"),
        P("gy"),
        P("gy"),
        P("gy", "gx"),
        P("gx"),
    )
    return jax.shard_map(
        functools.partial(per_device, mesh),
        mesh=mesh,
        in_specs=placed,
        out_specs=P(None, ("groups", "gy"), "gx"),
        check_vma=False,
    )
```
